128 devices in a mesh: frame: 4 (over y), head: 32 (over x, z, core).
Axes of the slice: x: 4, y: 4, z: 4, core: 2. Of those that a mesh axis runs over, the one named last changes fastest.
Arguments:
- queries: bfloat16 [6144, 4096], P(('frame', 'head'))
- keys: bfloat16 [6144, 4096], P(('frame', 'head'))
- values: bfloat16 [6144, 4096], P(('frame', 'head')), may hold values from -6 to 6
- grad_out: bfloat16 [6144, 4096], P(('frame', 'head')), may hold values from -48 to 48
- frame_order: int32 [8], replicated, may hold values from 0 to 7, each once
- key_blocks: int32 [48, 34], replicated, may hold values from 0 to 47, as said below
- key_count: int32 [48], replicated, may hold values from 12 to 34, as said below
Outputs:
- grad_queries: bfloat16 [6144, 4096], P(('frame', 'head'))
- grad_keys: bfloat16 [6144, 4096], P(('frame', 'head'))
- grad_values: bfloat16 [6144, 4096], P(('frame', 'head'))
The draws below stay inside these ranges and needn't reach their ends.
Inputs may be any that keep to these rules, and one draw needn't show every extreme that they name: `key_blocks`: row a lists, in its first key_count[a] entries, distinct key blocks in rising order; later entries are to be ignored. Every list holds all blocks of its own true frame and of the true frames next to it, and no block of a true frame more than 3 frames away. `key_count`: number of live entries of each row of key_blocks; at least the blocks of its own frame and one neighbouring frame.
All inputs are finite; a program needn't handle non-finite values.
Results may differ from the reference program's by a relative error of at most 0.017.
Values may be sent and summed in bfloat16 or wider, within the bound.
A program may use at most 64 MiB of HBM per device.

```python
import math
import jax
import jax.numpy as jnp
from jax import lax

HD = 128
HEADS = 32
D = 4096
FRAMES = 8
FRAME_TOK = 768
BLK = 128
LIST = 34
TOKENS = 6144


def draw_queries(key, part):
    key = jax.random.fold_in(key, 1)
    result = jnp.clip(jax.random.normal(key, (TOKENS, D)), -4.0, 4.0)
    return result.astype(jnp.bfloat16)


def draw_keys(key, part):
    key = jax.random.fold_in(key, 2)
    result = jnp.clip(jax.random.normal(key, (TOKENS, D)), -4.0, 4.0)
    return result.astype(jnp.bfloat16)


def radial_lists(key):
    per_frame = FRAME_TOK // BLK
    block_total = FRAMES * per_frame
    block_ids = jnp.arange(block_total, dtype=jnp.int32)
    frame_ids = block_ids // per_frame
    spot_ids = block_ids % per_frame
    jitter = jax.random.randint(jax.random.fold_in(key, 11), (block_total, FRAMES), 0, 2)
    forced_frame = jax.random.randint(jax.random.fold_in(key, 12), (), 3, FRAMES - 3)
    forced_block = forced_frame * per_frame + (per_frame - 1) // 2
    jitter = jnp.where(block_ids[:, None] == forced_block, 0, jitter)
    distance = jnp.abs(frame_ids[:, None] - frame_ids[None, :])
    jitter_pairs = jitter[:, frame_ids]
    reach = jnp.right_shift(jnp.int32(per_frame - 1), jnp.maximum(distance - 1, 0)) - jitter_pairs
    near = jnp.abs(spot_ids[:, None] - spot_ids[None, :]) <= reach
    allowed = (distance <= 1) | (distance <= 3) & near
    counts = jnp.sum(allowed.astype(jnp.int32), axis=1).astype(jnp.int32)
    ranking = jnp.where(allowed, block_ids[None, :], block_total + block_ids[None, :])
    ordered = jnp.argsort(ranking, axis=1, stable=True)[:, :LIST].astype(jnp.int32)
    filler = jax.random.randint(jax.random.fold_in(key, 13), (block_total, LIST), 0, block_total)
    slot_ids = jnp.arange(LIST, dtype=jnp.int32)[None, :]
    lists = jnp.where(slot_ids < counts[:, None], ordered, filler).astype(jnp.int32)
    return (lists, counts)


def draw_key_blocks(key, part):
    lists, counts = radial_lists(key)
    return lists


def draw_key_count(key, part):
    lists, counts = radial_lists(key)
    return counts


def block_levels(key, dims, pieces, smallest, high):
    factor_of = 1.0
    for position, blocks in pieces:
        steps = jax.random.uniform(jax.random.fold_in(jax.random.fold_in(key, 6), position), (blocks,), jnp.float32, smallest / len(pieces), high / len(pieces))
        factor_of = factor_of * jnp.repeat(jnp.exp(steps), dims[position] // blocks).reshape((-1,) + (1,) * (len(dims) - 1 - position))
    return factor_of


def gaussian(own_key, extent, scale, most, cuts=(), kind=jnp.bfloat16):
    values = scale * jax.random.normal(own_key, extent, jnp.float32)
    if cuts:
        values = values * block_levels(own_key, extent, cuts, -0.22, 0.18)
    return jnp.clip(values, -most, most).astype(kind)


def setup_inputs(seed: int = 0) -> dict:
    splits = jax.random.split(jax.random.key(seed), 8)
    return {
        "queries": draw_queries(jax.random.fold_in(splits[7], 71), 0),
        "keys": draw_keys(jax.random.fold_in(splits[7], 71), 0),
        "values": gaussian(splits[2], (TOKENS, D), 1.0, 6.0, ((0, 128),)),
        "grad_out": gaussian(splits[3], (TOKENS, D), 8.0, 48.0, ((0, 128),)),
        "frame_order": jax.random.permutation(splits[4], FRAMES).astype(jnp.int32),
        "key_blocks": draw_key_blocks(jax.random.fold_in(splits[7], 71), 0),
        "key_count": draw_key_count(jax.random.fold_in(splits[7], 71), 0),
    }


def block_table(key_blocks, key_count):
    block_total = key_blocks.shape[0]
    list_width = key_blocks.shape[1]
    live = jnp.arange(list_width, dtype=jnp.int32)[None, :] < key_count[:, None]
    hits = (key_blocks[:, :, None] == jnp.arange(block_total, dtype=jnp.int32)[None, None, :]) & live[:, :, None]
    return jnp.any(hits, axis=1).astype(jnp.float32)

def reference(queries, keys, values, grad_out, frame_order, key_blocks, key_count):
    allowed = block_table(key_blocks, key_count)
    per_frame = FRAME_TOK // BLK
    row_ids = jnp.arange(TOKENS, dtype=jnp.int32)
    rowblock = (frame_order[row_ids // FRAME_TOK] * per_frame + row_ids % FRAME_TOK // BLK).astype(jnp.int32)
    linked = allowed[rowblock][:, rowblock] > 0.5
    factor = 1.0 / math.sqrt(HD)

    def by_heads(array):
        return array.reshape(TOKENS, HEADS, HD).transpose(1, 0, 2)

    def one_head(parts):
        query, key_rows, value_rows, grad_rows = parts
        score = jnp.dot(query, key_rows.T, preferred_element_type=jnp.float32) * factor
        peak = lax.optimization_barrier(jnp.max(jnp.where(linked, score, -jnp.inf), axis=1))
        shifted = jnp.where(linked, jnp.exp(score - peak[:, None]), 0.0)
        lse = peak + jnp.log(lax.optimization_barrier(jnp.sum(shifted, axis=1)))
        weights = jnp.where(linked, jnp.exp(score - lse[:, None]), 0.0)
        weight_grads = jnp.dot(grad_rows, value_rows.T, preferred_element_type=jnp.float32)
        row_dot = lax.optimization_barrier(jnp.sum(weights * weight_grads, axis=1))
        score_grads = (weights * (weight_grads - row_dot[:, None])).astype(jnp.bfloat16)
        weights_b = weights.astype(jnp.bfloat16)
        grad_v = jnp.dot(weights_b.T, grad_rows, preferred_element_type=jnp.float32)
        grad_k = jnp.dot(score_grads.T, query, preferred_element_type=jnp.float32) * factor
        grad_q = jnp.dot(score_grads, key_rows, preferred_element_type=jnp.float32) * factor
        return (grad_q.astype(jnp.bfloat16), grad_k.astype(jnp.bfloat16), grad_v.astype(jnp.bfloat16))
    grad_q, grad_k, grad_v = lax.map(one_head, (by_heads(queries), by_heads(keys), by_heads(values), by_heads(grad_out)))

    def by_rows(array):
        return array.transpose(1, 0, 2).reshape(TOKENS, HEADS * HD)
    return (by_rows(grad_q), by_rows(grad_k), by_rows(grad_v))
```

```python
import jax
import jax.numpy as jnp
from jax import lax
from jax.experimental import pallas as pl
from jax.experimental.pallas import tpu as pltpu
from jax.sharding import PartitionSpec as P

HD = 128
FRAME_TOK = 768
BLK = 128
PER_FRAME = FRAME_TOK // BLK
NH = 32
NY = 4
RB = 48
HALF = NH * RB
TOTAL_BLOCKS = NY * HALF // BLK
HALF_BLOCKS = HALF // BLK
TQ = 512
NT = HALF // TQ
NQ = 2 * NT
FACTOR = HD**-0.5
LOG2E = 1.4426950408889634
SCALE = FACTOR * LOG2E
NEG = -1e30
MESH = pl.DeviceIdType.MESH

CONTRACT_LAST = (((1,), (1,)), ((), ()))
CONTRACT_FIRST = (((0,), (0,)), ((), ()))
CONTRACT_INNER = (((1,), (0,)), ((), ()))


def dot(a, b, dims):
    return lax.dot_general(a, b, dims, preferred_element_type=jnp.float32)


def cols(index):
    return pl.ds(pl.multiple_of(index * HD, HD), HD)


def block_rows(index):
    return pl.ds(pl.multiple_of(index * RB, RB), RB)


def tile_rows(index):
    return pl.ds(pl.multiple_of(index * TQ, TQ), TQ)


def kernel(
    q_in, k_in, v_in, g_in, order, lists, counts,
    dq_out, dk_out, dv_out,
    q_all, k_all, v_all, g_all,
    expo, wgrad, bias, peak, total, fac, rdot, dpart,
    ml_out, ml_in, d_out, d_in,
    dv_acc, dk_acc, dq_acc,
    dv_send, dk_send, dq_send, dv_recv, dk_recv, dq_recv, dv_fin, dk_fin, dq_fin,
    in_send, in_recv, in_local, y_send, y_recv, st_send, st_recv,
    part_send, part_recv, out_send, out_recv, out_local,
):
    y = lax.axis_index("frame")
    h = lax.axis_index("head")
    core = lax.rem(h, 2)
    low = y + 1 - 2 * lax.rem(y, 2)
    high = NY - 1 - y
    qp = (1 - core) * low + core * high
    kp = core * low + (1 - core) * high

    barrier = pltpu.get_barrier_semaphore()

    def greet(i, _):
        peer = lax.rem(h + i, NH)
        pl.semaphore_signal(barrier, inc=1, device_id=(y, peer), device_id_type=MESH)
        return 0

    lax.fori_loop(1, NH, greet, 0)
    pl.semaphore_signal(barrier, inc=1, device_id=(qp, h), device_id_type=MESH)
    pl.semaphore_signal(barrier, inc=1, device_id=(kp, h), device_id_type=MESH)
    pl.semaphore_wait(barrier, NH + 1)

    sources = (q_in, k_in, g_in, v_in)
    landing = (q_all, k_all, g_all, v_all)
    partner = (qp, kp, qp, kp)

    for a in range(4):
        src, dst = sources[a], landing[a]

        def send(i, _, src=src, dst=dst, a=a):
            peer = lax.rem(h + i, NH)
            pltpu.make_async_remote_copy(
                src_ref=src.at[:, cols(peer)],
                dst_ref=dst.at[block_rows(h), :],
                send_sem=in_send.at[a],
                recv_sem=in_recv.at[a],
                device_id=(y, peer),
                device_id_type=MESH,
            ).start()
            return 0

        lax.fori_loop(1, NH, send, 0)
        pltpu.make_async_copy(src.at[:, cols(h)], dst.at[block_rows(h), :], in_local.at[a]).start()

    def across(a):
        return pltpu.make_async_remote_copy(
            src_ref=landing[a].at[pl.ds(0, HALF), :],
            dst_ref=landing[a].at[pl.ds(HALF, HALF), :],
            send_sem=y_send.at[a],
            recv_sem=y_recv.at[a],
            device_id=(partner[a], h),
            device_id_type=MESH,
        )

    def own_arrived(a):
        src, dst = sources[a], landing[a]
        most = dst.at[pl.ds(0, HALF - RB), :]
        pltpu.make_async_copy(src.at[:, cols(h)], dst.at[block_rows(h), :], in_local.at[a]).wait()
        pltpu.make_async_copy(most, most, in_recv.at[a]).wait()
        across(a).start()

    block_ids = lax.broadcasted_iota(jnp.int32, (TOTAL_BLOCKS, TOTAL_BLOCKS), 1)
    row_ids = lax.broadcasted_iota(jnp.int32, (TOTAL_BLOCKS, TOTAL_BLOCKS), 0)
    live = jnp.sum(jnp.where(block_ids == row_ids, counts[...], 0), axis=1, keepdims=True)
    listed = lists[...]
    allowed = jnp.zeros((TOTAL_BLOCKS, TOTAL_BLOCKS), jnp.float32)
    for j in range(listed.shape[1]):
        hit = (listed[:, j : j + 1] == block_ids) & (live > j)
        allowed = jnp.where(hit, 1.0, allowed)

    def block_of(index, other):
        slot = index // PER_FRAME
        frame = jnp.where(
            slot < 2,
            jnp.where(slot == 0, order[2 * y], order[2 * y + 1]),
            jnp.where(slot == 2, order[2 * other], order[2 * other + 1]),
        )
        return frame * PER_FRAME + lax.rem(index, PER_FRAME)

    key_shape = (2 * HALF_BLOCKS, TOTAL_BLOCKS)
    key_index = lax.broadcasted_iota(jnp.int32, key_shape, 0)
    key_pick = (block_of(key_index, kp) == lax.broadcasted_iota(jnp.int32, key_shape, 1)).astype(jnp.float32)
    row_shape = (TOTAL_BLOCKS, 2 * HALF)
    row_index = lax.broadcasted_iota(jnp.int32, row_shape, 1) // BLK
    row_pick = (block_of(row_index, qp) == lax.broadcasted_iota(jnp.int32, row_shape, 0)).astype(jnp.float32)
    linked = dot(dot(key_pick, allowed, CONTRACT_LAST), row_pick, CONTRACT_INNER)
    offset = jnp.where(linked > 0.5, 0.0, NEG)
    for half in range(2):
        for i in range(NQ):
            for b in range(HALF_BLOCKS):
                row = half * HALF_BLOCKS + b
                bias[half, i, b] = offset[row : row + 1, i * TQ : (i + 1) * TQ]

    def scores(half, first, last):
        def step(i, _):
            s = dot(k_all[pl.ds(half * HALF, HALF), :], q_all[tile_rows(i), :], CONTRACT_LAST) * SCALE
            b = jnp.broadcast_to(bias[half, i], (HALF_BLOCKS, BLK, TQ)).reshape(HALF, TQ)
            s = s + b
            top = jnp.max(s, axis=0, keepdims=True)
            e = jnp.exp2(s - top).astype(jnp.bfloat16)
            expo[half, i] = e
            peak[half, i] = top
            total[half, i] = jnp.sum(e.astype(jnp.float32), axis=0, keepdims=True)
            return 0

        lax.fori_loop(first, last, step, 0)

    def weight_grads(half, first, last):
        def step(i, _):
            w = dot(v_all[pl.ds(half * HALF, HALF), :], g_all[tile_rows(i), :], CONTRACT_LAST)
            w = w.astype(jnp.bfloat16)
            wgrad[half, i] = w
            dpart[half, i] = jnp.sum(
                expo[half, i].astype(jnp.float32) * w.astype(jnp.float32), axis=0, keepdims=True
            )
            return 0

        lax.fori_loop(first, last, step, 0)

    def value_grads(half):
        dv_acc[half] = jnp.zeros((HALF, HD), jnp.float32)

        def step(i, _):
            p = (expo[half, i].astype(jnp.float32) * fac[half, i]).astype(jnp.bfloat16)
            dv_acc[half] += dot(p, g_all[tile_rows(i), :], CONTRACT_INNER)
            return 0

        lax.fori_loop(0, NQ, step, 0)

    def score_grads(half, first, last):
        def step(i, _):
            p = expo[half, i].astype(jnp.float32) * fac[half, i]
            ds = (p * (wgrad[half, i].astype(jnp.float32) - rdot[i])).astype(jnp.bfloat16)
            dk_acc[half] += dot(ds, q_all[tile_rows(i), :], CONTRACT_INNER)
            dq_acc[i] += dot(ds, k_all[pl.ds(half * HALF, HALF), :], CONTRACT_FIRST)
            return 0

        lax.fori_loop(first, last, step, 0)

    def stats(out, into, n):
        return pltpu.make_async_remote_copy(
            src_ref=out,
            dst_ref=into,
            send_sem=st_send.at[n],
            recv_sem=st_recv.at[n],
            device_id=(qp, h),
            device_id_type=MESH,
        )

    partials = ((dv_send, dv_recv, kp), (dk_send, dk_recv, kp), (dq_send, dq_recv, qp))

    def partial(n):
        out, into, peer = partials[n]
        return pltpu.make_async_remote_copy(
            src_ref=out,
            dst_ref=into,
            send_sem=part_send.at[n],
            recv_sem=part_recv.at[n],
            device_id=(peer, h),
            device_id_type=MESH,
        )

    finals = ((dv_fin, dv_out), (dk_fin, dk_out), (dq_fin, dq_out))

    def spread(n):
        fin, out = finals[n]

        def send(i, _):
            peer = lax.rem(h + i, NH)
            pltpu.make_async_remote_copy(
                src_ref=fin.at[block_rows(peer), :],
                dst_ref=out.at[:, cols(h)],
                send_sem=out_send.at[n],
                recv_sem=out_recv.at[n],
                device_id=(y, peer),
                device_id_type=MESH,
            ).start()
            return 0

        lax.fori_loop(1, NH, send, 0)
        pltpu.make_async_copy(fin.at[block_rows(h), :], out.at[:, cols(h)], out_local.at[n]).start()

    dk_acc[...] = jnp.zeros_like(dk_acc)
    dq_acc[...] = jnp.zeros_like(dq_acc)

    own_arrived(0)
    own_arrived(1)
    scores(0, 0, NT)
    across(0).wait()
    scores(0, NT, NQ)
    own_arrived(2)
    across(1).wait()
    scores(1, 0, NQ)

    top = jnp.maximum(peak[0], peak[1])
    ml_out[0] = top
    ml_out[1] = total[0] * jnp.exp2(peak[0] - top) + total[1] * jnp.exp2(peak[1] - top)
    stats(ml_out, ml_in, 0).start()
    own_arrived(3)
    weight_grads(0, 0, NT)
    across(2).wait()
    weight_grads(0, NT, NQ)
    stats(ml_out, ml_in, 0).wait()
    for i in range(NQ):
        j = (i + NT) % NQ
        here, there = ml_out[0, i], ml_in[0, j]
        top = jnp.maximum(here, there)
        norm = 1.0 / (ml_out[1, i] * jnp.exp2(here - top) + ml_in[1, j] * jnp.exp2(there - top))
        for half in range(2):
            fac[half, i] = jnp.exp2(peak[half, i] - top) * norm
    value_grads(1)
    dv_send[...] = dv_acc[1].astype(jnp.bfloat16)
    partial(0).start()
    across(3).wait()
    weight_grads(1, 0, NQ)
    for i in range(NQ):
        d_out[i] = dpart[0, i] * fac[0, i] + dpart[1, i] * fac[1, i]
    stats(d_out, d_in, 1).start()
    value_grads(0)
    stats(d_out, d_in, 1).wait()
    for i in range(NQ):
        rdot[i] = d_out[i] + d_in[(i + NT) % NQ]
    partial(0).wait()
    dv_fin[...] = (dv_acc[0] + dv_recv[...].astype(jnp.float32)).astype(jnp.bfloat16)
    spread(0)

    score_grads(1, 0, NQ)
    dk_send[...] = (dk_acc[1] * FACTOR).astype(jnp.bfloat16)
    partial(1).start()
    score_grads(0, NT, NQ)
    for i in range(NT):
        dq_send[pl.ds(i * TQ, TQ), :] = (dq_acc[NT + i] * FACTOR).astype(jnp.bfloat16)
    partial(2).start()
    score_grads(0, 0, NT)
    partial(1).wait()
    dk_fin[...] = (dk_acc[0] * FACTOR + dk_recv[...].astype(jnp.float32)).astype(jnp.bfloat16)
    spread(1)
    partial(2).wait()
    for i in range(NT):
        rows = pl.ds(i * TQ, TQ)
        dq_fin[rows, :] = (dq_acc[i] * FACTOR + dq_recv[rows, :].astype(jnp.float32)).astype(jnp.bfloat16)
    spread(2)

    for a in range(4):
        most = landing[a].at[pl.ds(0, HALF - RB), :]
        pltpu.make_async_copy(most, most, in_send.at[a]).wait()
    for n in range(3):
        fin, out = finals[n]
        sent = fin.at[pl.ds(0, HALF - RB), :]
        came = out.at[:, pl.ds(0, (NH - 1) * HD)]
        pltpu.make_async_copy(fin.at[block_rows(h), :], out.at[:, cols(h)], out_local.at[n]).wait()
        pltpu.make_async_copy(sent, sent, out_send.at[n]).wait()
        pltpu.make_async_copy(came, came, out_recv.at[n]).wait()


def shards(queries, keys, values, grad_out, frame_order, key_blocks, key_count):
    bf16, f32 = jnp.bfloat16, jnp.float32
    half = pltpu.VMEM((HALF, HD), bf16)
    whole = pltpu.VMEM((2 * HALF, HD), bf16)
    row = pltpu.VMEM((2, NQ, 1, TQ), f32)
    one = pltpu.VMEM((NQ, 1, TQ), f32)
    dma = pltpu.SemaphoreType.DMA
    anywhere = pl.BlockSpec(memory_space=pl.ANY)
    return pl.pallas_call(
        kernel,
        out_shape=[jax.ShapeDtypeStruct(queries.shape, bf16)] * 3,
        in_specs=[anywhere] * 4
        + [
            pl.BlockSpec(memory_space=pltpu.SMEM),
            pl.BlockSpec(memory_space=pltpu.VMEM),
            pl.BlockSpec(memory_space=pltpu.VMEM),
        ],
        out_specs=[anywhere] * 3,
        scratch_shapes=[whole] * 4
        + [
            pltpu.VMEM((2, NQ, HALF, TQ), bf16),
            pltpu.VMEM((2, NQ, HALF, TQ), bf16),
            pltpu.VMEM((2, NQ, HALF_BLOCKS, 1, TQ), f32),
            row, row, row, one, row,
            row, row, one, one,
            pltpu.VMEM((2, HALF, HD), f32),
            pltpu.VMEM((2, HALF, HD), f32),
            pltpu.VMEM((NQ, TQ, HD), f32),
        ]
        + [half] * 9
        + [
            dma((4,)), dma((4,)), dma((4,)), dma((4,)), dma((4,)),
            dma((2,)), dma((2,)),
            dma((3,)), dma((3,)), dma((3,)), dma((3,)), dma((3,)),
        ],
        compiler_params=pltpu.CompilerParams(
            collective_id=0, has_side_effects=True, vmem_limit_bytes=60 << 20
        ),
        cost_estimate=pl.CostEstimate(flops=12 * 10**9, bytes_accessed=8 << 20, transcendentals=10**7),
        name="attention_grads",
    )(queries, keys, values, grad_out, frame_order, key_blocks, key_count[None, :])


def solution(mesh):
    tokens = P(("frame", "head"), None)
    return jax.shard_map(
        shards,
        mesh=mesh,
        in_specs=(tokens,) * 4 + (P(),) * 3,
        out_specs=(tokens,) * 3,
        check_vma=False,
    )
```

```python
import jax
import jax.numpy as jnp
from jax import lax
from jax.experimental import pallas as pl
from jax.experimental.pallas import tpu as pltpu
from jax.sharding import PartitionSpec as P

HD = 128
FRAME_TOK = 768
BLK = 128
PER_FRAME = FRAME_TOK // BLK
NH = 32
NY = 4
RB = 48
HALF = NH * RB
CHUNKS = 4
CB = NH // CHUNKS
CR = CB * RB
STRIDE = 5
TQ = 768
NT = HALF // TQ
NQ = 2 * NT
KC = 256
NK = HALF // KC
SUB = 8
GR = 16
FACTOR = HD**-0.5
LOG2E = 1.4426950408889634
SCALE = FACTOR * LOG2E
NEG = -1e30
MESH = pl.DeviceIdType.MESH

CONTRACT_LAST = (((1,), (1,)), ((), ()))
CONTRACT_FIRST = (((0,), (0,)), ((), ()))
CONTRACT_INNER = (((1,), (0,)), ((), ()))


def dot(a, b, dims):
    return lax.dot_general(a, b, dims, preferred_element_type=jnp.float32)


def cols(index):
    return pl.ds(pl.multiple_of(index * HD, HD), HD)


def block_rows(index):
    return pl.ds(pl.multiple_of(index * RB, RB), RB)


def tile_rows(index):
    return pl.ds(pl.multiple_of(index * TQ, TQ), TQ)


def half_rows(index):
    return pl.ds(pl.multiple_of(index * HALF, HALF), HALF)


def kernel(
    q_in, k_in, v_in, g_in, order, lists, counts,
    dq_out, dk_out, dv_out,
    q_all, k_all, v_all, g_all, q_mask, k_mask,
    probs, wgrad, peak, total, top, norm, dsum, rdot,
    ml_out, ml_in, d_out, d_in,
    dv_acc, dk_acc, dq_acc,
    dv_send, dk_send, dq_send, dv_recv, dk_recv, dq_recv,
    in_send, in_recv, in_local, y_send, y_recv, st_send, st_recv,
    part_send, part_recv, out_send, out_recv, out_local,
):
    y = lax.axis_index("frame")
    h = lax.axis_index("head")
    core = lax.rem(h, 2)
    low = y + 1 - 2 * lax.rem(y, 2)
    high = NY - 1 - y
    qp = (1 - core) * low + core * high
    kp = core * low + (1 - core) * high
    first = NT * ((1 - core) * lax.rem(y, 2) + core * (y // 2))

    barrier = pltpu.get_barrier_semaphore()

    def greet(i, _):
        peer = lax.rem(h + i, NH)
        pl.semaphore_signal(barrier, inc=1, device_id=(y, peer), device_id_type=MESH)
        return 0

    lax.fori_loop(1, NH, greet, 0)
    pl.semaphore_signal(barrier, inc=1, device_id=(qp, h), device_id_type=MESH)
    pl.semaphore_signal(barrier, inc=1, device_id=(kp, h), device_id_type=MESH)
    pl.semaphore_wait(barrier, NH + 1)

    sources = (k_in, q_in, g_in, v_in)
    landing = (k_all, q_all, g_all, v_all)
    partner = (kp, qp, qp, kp)

    def own_block(a):
        return pltpu.make_async_copy(
            sources[a].at[:, cols(h)], landing[a].at[pl.ds(0, RB), :], in_local.at[a]
        )

    def regroup(a, c):
        def send(p, _):
            peer = lax.rem(h + STRIDE * p, NH)
            pltpu.make_async_remote_copy(
                src_ref=sources[a].at[:, cols(peer)],
                dst_ref=landing[a].at[block_rows(p), :],
                send_sem=in_send.at[a],
                recv_sem=in_recv.at[a, c],
                device_id=(y, peer),
                device_id_type=MESH,
            ).start()
            return 0

        lax.fori_loop(max(1, c * CB), (c + 1) * CB, send, 0)

    for a in range(4):
        own_block(a).start()
    for a in range(2):
        for c in range(CHUNKS):
            regroup(a, c)

    def across(a, c):
        return pltpu.make_async_remote_copy(
            src_ref=landing[a].at[pl.ds(c * CR, CR), :],
            dst_ref=landing[a].at[pl.ds(HALF + c * CR, CR), :],
            send_sem=y_send.at[a, c],
            recv_sem=y_recv.at[a, c],
            device_id=(partner[a], h),
            device_id_type=MESH,
        )

    def pass_on(a, c):
        if c == 0:
            own_block(a).wait()
        some = landing[a].at[pl.ds(0, (CB - (c == 0)) * RB), :]
        pltpu.make_async_copy(some, some, in_recv.at[a, c]).wait()
        across(a, c).start()

    def crossed(a):
        for c in range(CHUNKS):
            across(a, c).wait()

    shape = (HALF // GR, HD)
    row = lax.broadcasted_iota(jnp.int32, shape, 0) * GR
    lane = lax.broadcasted_iota(jnp.int32, shape, 1)
    place = row // RB
    holder = lax.rem(h - STRIDE * place + STRIDE * NH, NH)
    stored = holder * RB + row - place * RB
    later = stored >= FRAME_TOK
    spot = jnp.where(later, stored - FRAME_TOK, stored) // BLK

    def one_hot(plane):
        frame = jnp.where(later, order[2 * plane + 1], order[2 * plane])
        return (frame * PER_FRAME + spot == lane).astype(jnp.float32)

    def spell_out(groups):
        return jnp.broadcast_to(groups[:, None, :], (HALF // GR, GR, HD)).reshape(HALF, HD).astype(jnp.bfloat16)

    block_total = lists.shape[1]
    listed = lists[...]
    live = counts[...]
    ids = lax.broadcasted_iota(jnp.int32, (HD, block_total), 0)
    barred = jnp.full((HD, block_total), NEG, jnp.float32)
    for j in range(lists.shape[0]):
        barred = jnp.where((listed[j : j + 1, :] == ids) & (live > j), 0.0, barred)
    mine = one_hot(y)
    k_mask[pl.ds(0, HALF), :] = spell_out(mine)
    k_mask[pl.ds(HALF, HALF), :] = spell_out(one_hot(kp))
    for half, hot in ((0, mine), (1, one_hot(qp))):
        q_mask[pl.ds(half * HALF, HALF), :] = spell_out(dot(hot[:, :block_total], barred, CONTRACT_LAST))
    dv_acc[...] = jnp.zeros_like(dv_acc)
    dk_acc[...] = jnp.zeros_like(dk_acc)
    dq_acc[...] = jnp.zeros_like(dq_acc)
    dsum[...] = jnp.zeros_like(dsum)

    def turn(t):
        return lax.rem(t + first, NQ)

    def score_tile(half, i):
        q = jnp.concatenate([q_all[tile_rows(i), :], q_mask[tile_rows(i), :]], axis=1)

        def scores(c):
            keys = pl.ds(pl.multiple_of(half * HALF + c * KC, KC), KC)
            k = jnp.concatenate([k_all[keys, :], k_mask[keys, :]], axis=1)
            s = dot(k, q, CONTRACT_LAST).reshape(KC // SUB, SUB, TQ)
            return s, jnp.max(s, axis=0)

        s, high_s = scores(0)
        for c in range(NK):
            if c + 1 < NK:
                next_s, next_high = scores(c + 1)
            e = jnp.exp2((s - high_s[None]) * SCALE)
            probs[half, i, pl.ds(c * KC, KC)] = e.reshape(KC, TQ).astype(jnp.bfloat16)
            peak[half, i, c] = high_s
            total[half, i, c] = jnp.sum(e, axis=0)
            if c + 1 < NK:
                s, high_s = next_s, next_high

    def stats(n):
        return pltpu.make_async_remote_copy(
            src_ref=ml_out.at[n],
            dst_ref=ml_in.at[n],
            send_sem=st_send.at[n],
            recv_sem=st_recv.at[n],
            device_id=(qp, h),
            device_id_type=MESH,
        )

    def send_stats(n):
        for u in range(NT):
            i = turn(n * NT + u)
            p = jnp.maximum(peak[0, i], peak[1, i])
            best = jnp.max(jnp.max(p, axis=0), axis=0, keepdims=True)
            summed = total[0, i] * jnp.exp2((peak[0, i] - best) * SCALE) + total[1, i] * jnp.exp2(
                (peak[1, i] - best) * SCALE
            )
            ml_out[n, 0, u] = best
            ml_out[n, 1, u] = jnp.sum(jnp.sum(summed, axis=0), axis=0, keepdims=True)
        stats(n).start()

    def take_stats(n):
        stats(n).wait()
        for u in range(NT):
            i = turn(n * NT + u)
            here, there = ml_out[n, 0, u], ml_in[n, 0, u]
            best = jnp.maximum(here, there)
            top[i] = best
            norm[i] = 1.0 / (
                ml_out[n, 1, u] * jnp.exp2((here - best) * SCALE)
                + ml_in[n, 1, u] * jnp.exp2((there - best) * SCALE)
            )

    def normal(half, i):
        f = jnp.exp2((peak[half, i] - top[i][None]) * SCALE) * norm[i][None]
        e = probs[half, i].astype(jnp.float32).reshape(NK, KC // SUB, SUB, TQ)
        p = (e * f[:, None]).reshape(HALF, TQ).astype(jnp.bfloat16)
        probs[half, i] = p
        return p

    def weight_grads(half, i):
        p = probs[half, i]
        w = dot(v_all[half_rows(half), :], g_all[tile_rows(i), :], CONTRACT_LAST)
        wgrad[half, i] = w.astype(jnp.bfloat16)
        dsum[i] += jnp.sum((p.astype(jnp.float32) * w).reshape(HALF // SUB, SUB, TQ), axis=0)

    def score_grads(half, i):
        p = probs[half, i].astype(jnp.float32)
        ds = (p * (wgrad[half, i].astype(jnp.float32) - rdot[i])).astype(jnp.bfloat16)
        dk_acc[half] += dot(ds, q_all[tile_rows(i), :], CONTRACT_INNER)
        dq_acc[i] += dot(ds, k_all[half_rows(half), :], CONTRACT_FIRST)

    def share_rowdot(n):
        return pltpu.make_async_remote_copy(
            src_ref=d_out.at[n],
            dst_ref=d_in.at[n],
            send_sem=st_send.at[2 + n],
            recv_sem=st_recv.at[2 + n],
            device_id=(qp, h),
            device_id_type=MESH,
        )

    def partial(n):
        out, into, peer = (
            (dv_send, dv_recv, kp),
            (dk_send, dk_recv, kp),
            (dq_send.at[pl.ds(0, TQ), :], dq_recv.at[pl.ds(0, TQ), :], qp),
            (dq_send.at[pl.ds(TQ, TQ), :], dq_recv.at[pl.ds(TQ, TQ), :], qp),
        )[n]
        return pltpu.make_async_remote_copy(
            src_ref=out,
            dst_ref=into,
            send_sem=part_send.at[n],
            recv_sem=part_recv.at[n],
            device_id=(peer, h),
            device_id_type=MESH,
        )

    finals = ((dv_send, dv_out), (dk_send, dk_out), (dq_send, dq_out))

    def stay(n):
        fin, out = finals[n]
        return pltpu.make_async_copy(fin.at[pl.ds(0, RB), :], out.at[:, cols(h)], out_local.at[n])

    def spread(n, begin, end):
        fin, out = finals[n]

        def send(p, _):
            peer = lax.rem(h - STRIDE * p + STRIDE * NH, NH)
            pltpu.make_async_remote_copy(
                src_ref=fin.at[block_rows(p), :],
                dst_ref=out.at[:, cols(h)],
                send_sem=out_send.at[n],
                recv_sem=out_recv.at[n],
                device_id=(y, peer),
                device_id_type=MESH,
            ).start()
            return 0

        lax.fori_loop(max(1, begin), end, send, 0)
        if begin == 0:
            stay(n).start()

    for c in range(CHUNKS):
        pass_on(0, c)
        regroup(2, c)
    for c in range(CHUNKS // 2):
        pass_on(1, c)
        regroup(3, c)

    def score_step(t, _):
        half = t // NQ
        i = half * turn(t) + (1 - half) * t

        @pl.when(t == 1)
        def _():
            for c in range(CHUNKS // 2, CHUNKS):
                pass_on(1, c)
                regroup(3, c)

        @pl.when(t == NT)
        def _():
            crossed(1)

        @pl.when(t == NQ)
        def _():
            crossed(0)

        score_tile(half, i)
        for when, a, c in (
            (1, 2, 0), (2, 2, 1), (3, 2, 2), (3, 2, 3),
            (4, 3, 0), (5, 3, 1), (6, 3, 2), (7, 3, 3),
        ):

            @pl.when(t == when)
            def _(a=a, c=c):
                pass_on(a, c)

        @pl.when(t == NQ + NT - 1)
        def _():
            send_stats(0)

        return 0

    lax.fori_loop(0, 2 * NQ, score_step, 0)
    send_stats(1)
    crossed(2)

    def value_step(t, _):
        i = turn(t)
        half = 1 - t // NQ

        @pl.when(t == 0)
        def _():
            take_stats(0)

        @pl.when(t == NT)
        def _():
            take_stats(1)

        dv_acc[half] += dot(normal(half, i), g_all[tile_rows(i), :], CONTRACT_INNER)

        @pl.when(t == NQ - 1)
        def _():
            dv_send[...] = dv_acc[1].astype(jnp.bfloat16)
            partial(0).start()

        return 0

    lax.fori_loop(0, 2 * NQ, value_step, 0)
    crossed(3)

    def weight_step(t, _):
        weight_grads(lax.rem(t, 2), turn(t // 2))

        @pl.when(t == 0)
        def _():
            partial(0).wait()
            dv_send[...] = (dv_acc[0] + dv_recv[...].astype(jnp.float32)).astype(jnp.bfloat16)
            spread(0, 0, NH)

        for n in range(2):

            @pl.when(t == NQ * n + NQ - 1)
            def _(n=n):
                for u in range(NT):
                    d_out[n, u] = jnp.sum(dsum[turn(n * NT + u)], axis=0, keepdims=True)
                share_rowdot(n).start()

        return 0

    lax.fori_loop(0, 2 * NQ, weight_step, 0)

    def take_rowdot(n):
        share_rowdot(n).wait()
        for u in range(NT):
            rdot[turn(n * NT + u)] = d_out[n, u] + d_in[n, u]

    def finish_queries(i):
        rows = pl.ds(i * TQ, TQ)
        partial(2 + i).wait()
        dq_send[rows, :] = (dq_acc[i] * FACTOR + dq_recv[rows, :].astype(jnp.float32)).astype(jnp.bfloat16)
        spread(2, i * (NH // NT), (i + 1) * (NH // NT))

    near = first == 0

    def grad_step(t, _):
        half_near = jnp.where(t < 2, 1, jnp.where(t < 6, 1 - lax.rem(t, 2), 0))
        tile_near = jnp.where((t >= 2) & (t < 6), NT + (t - 2) // 2, lax.rem(t, NT))
        half_far = jnp.where((t < 2) | (t == 4) | (t == 5), 1, 0)
        tile_far = jnp.where(t < 4, NT, 0) + lax.rem(t, NT)
        half = jnp.where(near, half_near, half_far)
        i = jnp.where(near, tile_near, tile_far)
        for n in range(2):

            @pl.when(t == NT * n)
            def _(n=n):
                take_rowdot(n)

        score_grads(half, i)
        for u in range(NT):

            @pl.when(t == jnp.where(near, 3 + 2 * u, 2 + u))
            def _(u=u):
                dq_send[pl.ds(u * TQ, TQ), :] = (dq_acc[NT + u] * FACTOR).astype(jnp.bfloat16)
                partial(2 + u).start()

        @pl.when(t == jnp.where(near, 4, 5))
        def _():
            dk_send[...] = (dk_acc[1] * FACTOR).astype(jnp.bfloat16)
            partial(1).start()

        for u in range(NT):

            @pl.when(t == NQ + NT + u)
            def _(u=u):
                finish_queries(u)

        return 0

    lax.fori_loop(0, 2 * NQ, grad_step, 0)
    partial(1).wait()
    dk_send[...] = (dk_acc[0] * FACTOR + dk_recv[...].astype(jnp.float32)).astype(jnp.bfloat16)
    spread(1, 0, NH)

    for a in range(4):
        most = landing[a].at[pl.ds(0, HALF - RB), :]
        pltpu.make_async_copy(most, most, in_send.at[a]).wait()
    for n in range(3):
        fin, out = finals[n]
        sent = fin.at[pl.ds(0, HALF - RB), :]
        came = out.at[:, pl.ds(0, (NH - 1) * HD)]
        stay(n).wait()
        pltpu.make_async_copy(sent, sent, out_send.at[n]).wait()
        pltpu.make_async_copy(came, came, out_recv.at[n]).wait()


def shards(queries, keys, values, grad_out, frame_order, key_blocks, key_count):
    bf16, f32 = jnp.bfloat16, jnp.float32
    half = pltpu.VMEM((HALF, HD), bf16)
    whole = pltpu.VMEM((2 * HALF, HD), bf16)
    tiles = pltpu.VMEM((2, NQ, HALF, TQ), bf16)
    chunk_rows = pltpu.VMEM((2, NQ, NK, SUB, TQ), f32)
    line = pltpu.VMEM((NQ, 1, TQ), f32)
    pairs = pltpu.VMEM((2, 2, NT, 1, TQ), f32)
    pair = pltpu.VMEM((2, NT, 1, TQ), f32)
    dma = pltpu.SemaphoreType.DMA
    anywhere = pl.BlockSpec(memory_space=pl.ANY)
    return pl.pallas_call(
        kernel,
        out_shape=[jax.ShapeDtypeStruct(queries.shape, bf16)] * 3,
        in_specs=[anywhere] * 4
        + [
            pl.BlockSpec(memory_space=pltpu.SMEM),
            pl.BlockSpec(memory_space=pltpu.VMEM),
            pl.BlockSpec(memory_space=pltpu.VMEM),
        ],
        out_specs=[anywhere] * 3,
        scratch_shapes=[whole] * 6
        + [tiles] * 2
        + [chunk_rows] * 2
        + [line, line, pltpu.VMEM((NQ, SUB, TQ), f32), line]
        + [pairs, pairs, pair, pair]
        + [
            pltpu.VMEM((2, HALF, HD), f32),
            pltpu.VMEM((2, HALF, HD), f32),
            pltpu.VMEM((NQ, TQ, HD), f32),
        ]
        + [half] * 6
        + [
            dma((4,)), dma((4, CHUNKS)), dma((4,)), dma((4, CHUNKS)), dma((4, CHUNKS)),
            dma((4,)), dma((4,)),
            dma((4,)), dma((4,)), dma((3,)), dma((3,)), dma((3,)),
        ],
        compiler_params=pltpu.CompilerParams(
            collective_id=0, has_side_effects=True, vmem_limit_bytes=63 << 20
        ),
        cost_estimate=pl.CostEstimate(flops=12 * 10**9, bytes_accessed=8 << 20, transcendentals=10**7),
        name="attention_grads",
    )(queries, keys, values, grad_out, frame_order, key_blocks.T, key_count[None, :])


def solution(mesh):
    tokens = P(("frame", "head"), None)
    return jax.shard_map(
        shards,
        mesh=mesh,
        in_specs=(tokens,) * 4 + (P(),) * 3,
        out_specs=(tokens,) * 3,
        check_vma=False,
    )
```

```python
import jax
import jax.numpy as jnp
from jax import lax
from jax.experimental import pallas as pl
from jax.experimental.pallas import tpu as pltpu
from jax.sharding import PartitionSpec as P

HD = 128
FRAME_TOK = 768
BLK = 128
PER_FRAME = FRAME_TOK // BLK
NH = 32
NY = 4
RB = 48
HALF = NH * RB
CHUNKS = 4
CB = NH // CHUNKS
CR = CB * RB
STRIDE = 5
TQ = 768
NT = HALF // TQ
NQ = 2 * NT
KC = 256
NK = HALF // KC
SUB = 8
GR = 16
FACTOR = HD**-0.5
LOG2E = 1.4426950408889634
SCALE = FACTOR * LOG2E
NEG = -1e30
MESH = pl.DeviceIdType.MESH

CONTRACT_LAST = (((1,), (1,)), ((), ()))
CONTRACT_FIRST = (((0,), (0,)), ((), ()))
CONTRACT_INNER = (((1,), (0,)), ((), ()))


def dot(a, b, dims):
    return lax.dot_general(a, b, dims, preferred_element_type=jnp.float32)


def cols(index):
    return pl.ds(pl.multiple_of(index * HD, HD), HD)


def block_rows(index):
    return pl.ds(pl.multiple_of(index * RB, RB), RB)


def tile_rows(index):
    return pl.ds(pl.multiple_of(index * TQ, TQ), TQ)


def half_rows(index):
    return pl.ds(pl.multiple_of(index * HALF, HALF), HALF)


def kernel(
    q_in, k_in, v_in, g_in, order, lists, counts,
    dq_out, dk_out, dv_out,
    q_all, k_all, v_all, g_all, q_mask, k_mask,
    probs, wgrad, peak, total, top, norm, dsum, rdot,
    ml_out, ml_in, d_out, d_in,
    dv_acc, dk_acc, dq_acc,
    dv_send, dk_send, dq_send, dv_recv, dk_recv, dq_recv,
    in_send, in_recv, in_local, y_send, y_recv, st_send, st_recv,
    part_send, part_recv, out_send, out_recv, out_local,
):
    y = lax.axis_index("frame")
    h = lax.axis_index("head")
    core = lax.rem(h, 2)
    low = y + 1 - 2 * lax.rem(y, 2)
    high = NY - 1 - y
    qp = (1 - core) * low + core * high
    kp = core * low + (1 - core) * high
    first = NT * ((1 - core) * lax.rem(y, 2) + core * (y // 2))

    barrier = pltpu.get_barrier_semaphore()

    def greet(i, _):
        peer = lax.rem(h + i, NH)
        pl.semaphore_signal(barrier, inc=1, device_id=(y, peer), device_id_type=MESH)
        return 0

    lax.fori_loop(1, NH, greet, 0)
    pl.semaphore_signal(barrier, inc=1, device_id=(qp, h), device_id_type=MESH)
    pl.semaphore_signal(barrier, inc=1, device_id=(kp, h), device_id_type=MESH)
    pl.semaphore_wait(barrier, NH + 1)

    sources = (k_in, q_in, g_in, v_in)
    landing = (k_all, q_all, g_all, v_all)
    partner = (kp, qp, qp, kp)

    def own_block(a):
        return pltpu.make_async_copy(
            sources[a].at[:, cols(h)], landing[a].at[pl.ds(0, RB), :], in_local.at[a]
        )

    def regroup(a, c):
        def send(p, _):
            peer = lax.rem(h + STRIDE * p, NH)
            pltpu.make_async_remote_copy(
                src_ref=sources[a].at[:, cols(peer)],
                dst_ref=landing[a].at[block_rows(p), :],
                send_sem=in_send.at[a],
                recv_sem=in_recv.at[a, c],
                device_id=(y, peer),
                device_id_type=MESH,
            ).start()
            return 0

        lax.fori_loop(max(1, c * CB), (c + 1) * CB, send, 0)

    for a in range(4):
        own_block(a).start()
    for a in range(2):
        for c in range(CHUNKS):
            regroup(a, c)

    def across(a, c):
        return pltpu.make_async_remote_copy(
            src_ref=landing[a].at[pl.ds(c * CR, CR), :],
            dst_ref=landing[a].at[pl.ds(HALF + c * CR, CR), :],
            send_sem=y_send.at[a, c],
            recv_sem=y_recv.at[a, c],
            device_id=(partner[a], h),
            device_id_type=MESH,
        )

    def pass_on(a, c):
        if c == 0:
            own_block(a).wait()
        some = landing[a].at[pl.ds(0, (CB - (c == 0)) * RB), :]
        pltpu.make_async_copy(some, some, in_recv.at[a, c]).wait()
        across(a, c).start()

    def crossed(a):
        for c in range(CHUNKS):
            across(a, c).wait()

    shape = (HALF // GR, HD)
    row = lax.broadcasted_iota(jnp.int32, shape, 0) * GR
    lane = lax.broadcasted_iota(jnp.int32, shape, 1)
    place = row // RB
    holder = lax.rem(h - STRIDE * place + STRIDE * NH, NH)
    stored = holder * RB + row - place * RB
    later = stored >= FRAME_TOK
    spot = jnp.where(later, stored - FRAME_TOK, stored) // BLK

    def one_hot(plane):
        frame = jnp.where(later, order[2 * plane + 1], order[2 * plane])
        return (frame * PER_FRAME + spot == lane).astype(jnp.float32)

    def spell_out(groups):
        return jnp.broadcast_to(groups[:, None, :], (HALF // GR, GR, HD)).reshape(HALF, HD).astype(jnp.bfloat16)

    block_total = lists.shape[1]
    listed = lists[...]
    live = counts[...]
    ids = lax.broadcasted_iota(jnp.int32, (HD, block_total), 0)
    barred = jnp.full((HD, block_total), NEG, jnp.float32)
    for j in range(lists.shape[0]):
        barred = jnp.where((listed[j : j + 1, :] == ids) & (live > j), 0.0, barred)
    mine = one_hot(y)
    k_mask[pl.ds(0, HALF), :] = spell_out(mine)
    k_mask[pl.ds(HALF, HALF), :] = spell_out(one_hot(kp))
    for half, hot in ((0, mine), (1, one_hot(qp))):
        q_mask[pl.ds(half * HALF, HALF), :] = spell_out(dot(hot[:, :block_total], barred, CONTRACT_LAST))
    dv_acc[...] = jnp.zeros_like(dv_acc)
    dk_acc[...] = jnp.zeros_like(dk_acc)
    dq_acc[...] = jnp.zeros_like(dq_acc)
    dsum[...] = jnp.zeros_like(dsum)

    def turn(t):
        return lax.rem(t + first, NQ)

    def score_tile(half, i):
        q = jnp.concatenate([q_all[tile_rows(i), :], q_mask[tile_rows(i), :]], axis=1)

        def scores(c):
            keys = pl.ds(pl.multiple_of(half * HALF + c * KC, KC), KC)
            k = jnp.concatenate([k_all[keys, :], k_mask[keys, :]], axis=1)
            s = dot(k, q, CONTRACT_LAST).reshape(KC // SUB, SUB, TQ)
            return s, jnp.max(s, axis=0)

        s, high_s = scores(0)
        for c in range(NK):
            if c + 1 < NK:
                next_s, next_high = scores(c + 1)
            e = jnp.exp2((s - high_s[None]) * SCALE)
            probs[half, i, pl.ds(c * KC, KC)] = e.reshape(KC, TQ).astype(jnp.bfloat16)
            peak[half, i, c] = high_s
            total[half, i, c] = jnp.sum(e, axis=0)
            if c + 1 < NK:
                s, high_s = next_s, next_high

    def stats():
        return pltpu.make_async_remote_copy(
            src_ref=ml_out,
            dst_ref=ml_in,
            send_sem=st_send.at[2],
            recv_sem=st_recv.at[2],
            device_id=(qp, h),
            device_id_type=MESH,
        )

    def send_stats():
        for i in range(NQ):
            p = jnp.maximum(peak[0, i], peak[1, i])
            best = jnp.max(jnp.max(p, axis=0), axis=0, keepdims=True)
            summed = total[0, i] * jnp.exp2((peak[0, i] - best) * SCALE) + total[1, i] * jnp.exp2(
                (peak[1, i] - best) * SCALE
            )
            ml_out[0, i] = best
            ml_out[1, i] = jnp.sum(jnp.sum(summed, axis=0), axis=0, keepdims=True)
        stats().start()

    def take_stats():
        stats().wait()
        for i in range(NQ):
            j = (i + NT) % NQ
            here, there = ml_out[0, i], ml_in[0, j]
            best = jnp.maximum(here, there)
            top[i] = best
            norm[i] = 1.0 / (
                ml_out[1, i] * jnp.exp2((here - best) * SCALE) + ml_in[1, j] * jnp.exp2((there - best) * SCALE)
            )

    def normal(half, i):
        f = jnp.exp2((peak[half, i] - top[i][None]) * SCALE) * norm[i][None]
        e = probs[half, i].astype(jnp.float32).reshape(NK, KC // SUB, SUB, TQ)
        p = (e * f[:, None]).reshape(HALF, TQ).astype(jnp.bfloat16)
        probs[half, i] = p
        return p

    def weight_tile(half, i):
        return dot(v_all[half_rows(half), :], g_all[tile_rows(i), :], CONTRACT_LAST)

    def add_rowdot(i, p, w):
        dsum[i] += jnp.sum((p.astype(jnp.float32) * w).reshape(HALF // SUB, SUB, TQ), axis=0)

    def score_grads(half, i):
        p = probs[half, i].astype(jnp.float32)
        ds = (p * (wgrad[half, i].astype(jnp.float32) - rdot[i])).astype(jnp.bfloat16)
        dk_acc[half] += dot(ds, q_all[tile_rows(i), :], CONTRACT_INNER)
        dq_acc[i] += dot(ds, k_all[half_rows(half), :], CONTRACT_FIRST)

    def share_rowdot(n):
        return pltpu.make_async_remote_copy(
            src_ref=d_out.at[n],
            dst_ref=d_in.at[n],
            send_sem=st_send.at[n],
            recv_sem=st_recv.at[n],
            device_id=(qp, h),
            device_id_type=MESH,
        )

    def partial(n):
        out, into, peer = (
            (dv_send, dv_recv, kp),
            (dk_send, dk_recv, kp),
            (dq_send.at[pl.ds(0, TQ), :], dq_recv.at[pl.ds(0, TQ), :], qp),
            (dq_send.at[pl.ds(TQ, TQ), :], dq_recv.at[pl.ds(TQ, TQ), :], qp),
        )[n]
        return pltpu.make_async_remote_copy(
            src_ref=out,
            dst_ref=into,
            send_sem=part_send.at[n],
            recv_sem=part_recv.at[n],
            device_id=(peer, h),
            device_id_type=MESH,
        )

    def key_part(c):
        rows = pl.ds(c * CR, CR)
        return pltpu.make_async_remote_copy(
            src_ref=dk_send.at[rows, :],
            dst_ref=dk_recv.at[rows, :],
            send_sem=part_send.at[4 + c],
            recv_sem=part_recv.at[4 + c],
            device_id=(kp, h),
            device_id_type=MESH,
        )

    finals = ((dv_send, dv_out), (dk_send, dk_out), (dq_send, dq_out))

    def stay(n):
        fin, out = finals[n]
        return pltpu.make_async_copy(fin.at[pl.ds(0, RB), :], out.at[:, cols(h)], out_local.at[n])

    def spread(n, begin, end):
        fin, out = finals[n]

        def send(p, _):
            peer = lax.rem(h - STRIDE * p + STRIDE * NH, NH)
            pltpu.make_async_remote_copy(
                src_ref=fin.at[block_rows(p), :],
                dst_ref=out.at[:, cols(h)],
                send_sem=out_send.at[n],
                recv_sem=out_recv.at[n],
                device_id=(y, peer),
                device_id_type=MESH,
            ).start()
            return 0

        lax.fori_loop(max(1, begin), end, send, 0)
        if begin == 0:
            stay(n).start()

    for c in range(CHUNKS):
        pass_on(0, c)
        regroup(2, c)
    for c in range(CHUNKS // 2):
        pass_on(1, c)
        regroup(3, c)

    def score_step(t, _):
        half = lax.rem(t // NT, 2)
        i = NT * (t // NQ) + lax.rem(t, NT)

        @pl.when(t == 1)
        def _():
            for c in range(CHUNKS // 2, CHUNKS):
                pass_on(1, c)
                regroup(3, c)

        @pl.when(t == NT)
        def _():
            crossed(0)

        @pl.when(t == NQ)
        def _():
            crossed(1)

        score_tile(half, i)
        for when, a, c in (
            (1, 2, 0), (2, 2, 1), (3, 2, 2), (3, 2, 3),
            (4, 3, 0), (5, 3, 1), (5, 3, 2), (6, 3, 3),
        ):

            @pl.when(t == when)
            def _(a=a, c=c):
                pass_on(a, c)

        return 0

    lax.fori_loop(0, 2 * NQ, score_step, 0)
    send_stats()

    def near_weight_step(i, _):
        @pl.when(i == NT)
        def _():
            crossed(2)

        wgrad[0, i] = weight_tile(0, i).astype(jnp.bfloat16)
        return 0

    lax.fori_loop(0, NQ, near_weight_step, 0)
    take_stats()

    crossed(3)

    def far_step(i, _):
        w = weight_tile(1, i)
        wgrad[1, i] = w.astype(jnp.bfloat16)
        p = normal(1, i)
        add_rowdot(i, p, w)
        dv_acc[1] += dot(p, g_all[tile_rows(i), :], CONTRACT_INNER)
        return 0

    lax.fori_loop(0, NQ, far_step, 0)
    dv_send[...] = dv_acc[1].astype(jnp.bfloat16)
    partial(0).start()

    def near_step(t, _):
        i = turn(t)
        p = normal(0, i)
        add_rowdot(i, p, wgrad[0, i].astype(jnp.float32))
        dv_acc[0] += dot(p, g_all[tile_rows(i), :], CONTRACT_INNER)
        for n in range(2):

            @pl.when(t == NT * n + NT - 1)
            def _(n=n):
                for u in range(NT):
                    d_out[n, u] = jnp.sum(dsum[turn(n * NT + u)], axis=0, keepdims=True)
                share_rowdot(n).start()

        return 0

    lax.fori_loop(0, NQ, near_step, 0)

    def take_rowdot(n):
        share_rowdot(n).wait()
        for u in range(NT):
            rdot[turn(n * NT + u)] = d_out[n, u] + d_in[n, u]

    def finish_queries(i):
        rows = pl.ds(i * TQ, TQ)
        partial(2 + i).wait()
        dq_send[rows, :] = (dq_acc[i] * FACTOR + dq_recv[rows, :].astype(jnp.float32)).astype(jnp.bfloat16)
        spread(2, i * (NH // NT), (i + 1) * (NH // NT))

    near = first == 0

    def grad_step(t, _):
        half_near = jnp.where((t == 0) | (t == 1) | (t == 3) | (t == 5), 1, 0)
        tile_near = jnp.where((t >= 1) & (t < 5), NT + (t - 1) // 2, jnp.where((t == 0) | (t == 6), 0, 1))
        half_far = jnp.where((t == 0) | (t == 2) | (t == 4) | (t == 5), 1, 0)
        tile_far = jnp.where(t < 4, NT + t // 2, lax.rem(t, NT))
        half = jnp.where(near, half_near, half_far)
        i = jnp.where(near, tile_near, tile_far)

        @pl.when(t == 0)
        def _():
            take_rowdot(0)

        @pl.when(t == jnp.where(near, 1, 4))
        def _():
            take_rowdot(1)

        score_grads(half, i)

        @pl.when(t == 0)
        def _():
            partial(0).wait()
            dv_send[...] = (dv_acc[0] + dv_recv[...].astype(jnp.float32)).astype(jnp.bfloat16)
            spread(0, 0, NH)

        for u in range(NT):

            @pl.when(t == jnp.where(near, 2 + 2 * u, 1 + 2 * u))
            def _(u=u):
                dq_send[pl.ds(u * TQ, TQ), :] = (dq_acc[NT + u] * FACTOR).astype(jnp.bfloat16)
                partial(2 + u).start()

        @pl.when(t == 5)
        def _():
            dk_send[...] = (dk_acc[1] * FACTOR).astype(jnp.bfloat16)
            for c in range(CHUNKS):
                key_part(c).start()

        for u in range(NT):

            @pl.when(t == NQ + NT + u)
            def _(u=u):
                finish_queries(u)

        return 0

    lax.fori_loop(0, 2 * NQ, grad_step, 0)
    for c in range(CHUNKS):
        rows = pl.ds(c * CR, CR)
        key_part(c).wait()
        dk_send[rows, :] = (dk_acc[0, rows] * FACTOR + dk_recv[rows, :].astype(jnp.float32)).astype(jnp.bfloat16)
        spread(1, c * CB, (c + 1) * CB)

    for a in range(4):
        most = landing[a].at[pl.ds(0, HALF - RB), :]
        pltpu.make_async_copy(most, most, in_send.at[a]).wait()
    for n in range(3):
        fin, out = finals[n]
        sent = fin.at[pl.ds(0, HALF - RB), :]
        came = out.at[:, pl.ds(0, (NH - 1) * HD)]
        stay(n).wait()
        pltpu.make_async_copy(sent, sent, out_send.at[n]).wait()
        pltpu.make_async_copy(came, came, out_recv.at[n]).wait()


def shards(queries, keys, values, grad_out, frame_order, key_blocks, key_count):
    bf16, f32 = jnp.bfloat16, jnp.float32
    half = pltpu.VMEM((HALF, HD), bf16)
    whole = pltpu.VMEM((2 * HALF, HD), bf16)
    tiles = pltpu.VMEM((2, NQ, HALF, TQ), bf16)
    chunk_rows = pltpu.VMEM((2, NQ, NK, SUB, TQ), f32)
    line = pltpu.VMEM((NQ, 1, TQ), f32)
    pairs = pltpu.VMEM((2, NQ, 1, TQ), f32)
    pair = pltpu.VMEM((2, NT, 1, TQ), f32)
    dma = pltpu.SemaphoreType.DMA
    anywhere = pl.BlockSpec(memory_space=pl.ANY)
    return pl.pallas_call(
        kernel,
        out_shape=[jax.ShapeDtypeStruct(queries.shape, bf16)] * 3,
        in_specs=[anywhere] * 4
        + [
            pl.BlockSpec(memory_space=pltpu.SMEM),
            pl.BlockSpec(memory_space=pltpu.VMEM),
            pl.BlockSpec(memory_space=pltpu.VMEM),
        ],
        out_specs=[anywhere] * 3,
        scratch_shapes=[whole] * 6
        + [tiles] * 2
        + [chunk_rows] * 2
        + [line, line, pltpu.VMEM((NQ, SUB, TQ), f32), line]
        + [pairs, pairs, pair, pair]
        + [
            pltpu.VMEM((2, HALF, HD), f32),
            pltpu.VMEM((2, HALF, HD), f32),
            pltpu.VMEM((NQ, TQ, HD), f32),
        ]
        + [half] * 6
        + [
            dma((4,)), dma((4, CHUNKS)), dma((4,)), dma((4, CHUNKS)), dma((4, CHUNKS)),
            dma((3,)), dma((3,)),
            dma((4 + CHUNKS,)), dma((4 + CHUNKS,)), dma((3,)), dma((3,)), dma((3,)),
        ],
        compiler_params=pltpu.CompilerParams(
            collective_id=0, has_side_effects=True, vmem_limit_bytes=63 << 20
        ),
        cost_estimate=pl.CostEstimate(flops=12 * 10**9, bytes_accessed=8 << 20, transcendentals=10**7),
        name="attention_grads",
    )(queries, keys, values, grad_out, frame_order, key_blocks.T, key_count[None, :])


def solution(mesh):
    tokens = P(("frame", "head"), None)
    return jax.shard_map(
        shards,
        mesh=mesh,
        in_specs=(tokens,) * 4 + (P(),) * 3,
        out_specs=(tokens,) * 3,
        check_vma=False,
    )
```

```python
import jax
import jax.numpy as jnp
from jax import lax
from jax.experimental import pallas as pl
from jax.experimental.pallas import tpu as pltpu
from jax.sharding import PartitionSpec as P

HD = 128
FRAME_TOK = 768
BLK = 128
PER_FRAME = FRAME_TOK // BLK
NH = 32
NY = 4
RB = 48
HALF = NH * RB
CHUNKS = 4
CB = NH // CHUNKS
CR = CB * RB
STRIDE = 5
TQ = 768
NT = HALF // TQ
NQ = 2 * NT
KC = 256
NK = HALF // KC
SUB = 8
GR = 16
FACTOR = HD**-0.5
LOG2E = 1.4426950408889634
SCALE = FACTOR * LOG2E
NEG = -1e30
MESH = pl.DeviceIdType.MESH

CONTRACT_LAST = (((1,), (1,)), ((), ()))
CONTRACT_FIRST = (((0,), (0,)), ((), ()))
CONTRACT_INNER = (((1,), (0,)), ((), ()))


def dot(a, b, dims):
    return lax.dot_general(a, b, dims, preferred_element_type=jnp.float32)


def cols(index):
    return pl.ds(pl.multiple_of(index * HD, HD), HD)


def block_rows(index):
    return pl.ds(pl.multiple_of(index * RB, RB), RB)


def tile_rows(index):
    return pl.ds(pl.multiple_of(index * TQ, TQ), TQ)


def half_rows(index):
    return pl.ds(pl.multiple_of(index * HALF, HALF), HALF)


def kernel(
    q_in, k_in, v_in, g_in, order, lists, counts,
    dq_out, dk_out, dv_out,
    q_all, k_all, v_all, g_all, q_mask, k_mask,
    probs, wgrad, peak, tops, total, top, norm, dsum, rdot,
    ml_out, ml_in, d_out, d_in,
    dv_acc, dk_acc, dq_acc,
    dv_send, dk_send, dq_send, dv_recv, dk_recv, dq_recv,
    in_send, in_recv, in_local, y_send, y_recv, st_send, st_recv,
    part_send, part_recv, out_send, out_recv, out_local,
):
    y = lax.axis_index("frame")
    h = lax.axis_index("head")
    core = lax.rem(h, 2)
    low = y + 1 - 2 * lax.rem(y, 2)
    high = NY - 1 - y
    qp = (1 - core) * low + core * high
    kp = core * low + (1 - core) * high
    barrier = pltpu.get_barrier_semaphore()

    def greet(i, _):
        peer = lax.rem(h + i, NH)
        pl.semaphore_signal(barrier, inc=1, device_id=(y, peer), device_id_type=MESH)
        return 0

    lax.fori_loop(1, NH, greet, 0)
    pl.semaphore_signal(barrier, inc=1, device_id=(qp, h), device_id_type=MESH)
    pl.semaphore_signal(barrier, inc=1, device_id=(kp, h), device_id_type=MESH)
    pl.semaphore_wait(barrier, NH + 1)

    sources = (k_in, q_in, g_in, v_in)
    landing = (k_all, q_all, g_all, v_all)
    partner = (kp, qp, qp, kp)

    def own_block(a):
        return pltpu.make_async_copy(
            sources[a].at[:, cols(h)], landing[a].at[pl.ds(0, RB), :], in_local.at[a]
        )

    def regroup(a, c):
        def send(p, _):
            peer = lax.rem(h + STRIDE * p, NH)
            pltpu.make_async_remote_copy(
                src_ref=sources[a].at[:, cols(peer)],
                dst_ref=landing[a].at[block_rows(p), :],
                send_sem=in_send.at[a],
                recv_sem=in_recv.at[a, c],
                device_id=(y, peer),
                device_id_type=MESH,
            ).start()
            return 0

        lax.fori_loop(max(1, c * CB), (c + 1) * CB, send, 0)

    for a in range(4):
        own_block(a).start()
    for a in range(2):
        for c in range(CHUNKS):
            regroup(a, c)

    def across(a, c):
        return pltpu.make_async_remote_copy(
            src_ref=landing[a].at[pl.ds(c * CR, CR), :],
            dst_ref=landing[a].at[pl.ds(HALF + c * CR, CR), :],
            send_sem=y_send.at[a, c],
            recv_sem=y_recv.at[a, c],
            device_id=(partner[a], h),
            device_id_type=MESH,
        )

    def pass_on(a, c):
        if c == 0:
            own_block(a).wait()
        some = landing[a].at[pl.ds(0, (CB - (c == 0)) * RB), :]
        pltpu.make_async_copy(some, some, in_recv.at[a, c]).wait()
        across(a, c).start()

    def crossed(a):
        for c in range(CHUNKS):
            across(a, c).wait()

    shape = (HALF // GR, HD)
    row = lax.broadcasted_iota(jnp.int32, shape, 0) * GR
    lane = lax.broadcasted_iota(jnp.int32, shape, 1)
    place = row // RB
    holder = lax.rem(h - STRIDE * place + STRIDE * NH, NH)
    stored = holder * RB + row - place * RB
    later = stored >= FRAME_TOK
    spot = jnp.where(later, stored - FRAME_TOK, stored) // BLK

    def one_hot(plane):
        frame = jnp.where(later, order[2 * plane + 1], order[2 * plane])
        return (frame * PER_FRAME + spot == lane).astype(jnp.float32)

    def spell_out(groups):
        return jnp.broadcast_to(groups[:, None, :], (HALF // GR, GR, HD)).reshape(HALF, HD).astype(jnp.bfloat16)

    block_total = lists.shape[1]
    listed = lists[...]
    live = counts[...]
    ids = lax.broadcasted_iota(jnp.int32, (HD, block_total), 0)
    barred = jnp.full((HD, block_total), NEG, jnp.float32)
    for j in range(lists.shape[0]):
        barred = jnp.where((listed[j : j + 1, :] == ids) & (live > j), 0.0, barred)
    mine = one_hot(y)
    k_mask[pl.ds(0, HALF), :] = spell_out(mine)
    k_mask[pl.ds(HALF, HALF), :] = spell_out(one_hot(kp))
    for half, hot in ((0, mine), (1, one_hot(qp))):
        q_mask[pl.ds(half * HALF, HALF), :] = spell_out(dot(hot[:, :block_total], barred, CONTRACT_LAST))
    dv_acc[...] = jnp.zeros_like(dv_acc)
    dk_acc[...] = jnp.zeros_like(dk_acc)
    dq_acc[...] = jnp.zeros_like(dq_acc)
    dsum[...] = jnp.zeros_like(dsum)

    def score_tile(half, i):
        q = jnp.concatenate([q_all[tile_rows(i), :], q_mask[tile_rows(i), :]], axis=1)

        def scores(c):
            keys = pl.ds(pl.multiple_of(half * HALF + c * KC, KC), KC)
            k = jnp.concatenate([k_all[keys, :], k_mask[keys, :]], axis=1)
            s = dot(k, q, CONTRACT_LAST).reshape(KC // SUB, SUB, TQ)
            return s, jnp.max(s, axis=0)

        s, high_s = scores(0)
        sums = []
        for c in range(NK):
            if c + 1 < NK:
                next_s, next_high = scores(c + 1)
            e = jnp.exp2((s - high_s[None]) * SCALE)
            probs[half, i, pl.ds(c * KC, KC)] = e.reshape(KC, TQ).astype(jnp.bfloat16)
            peak[half, i, c] = high_s
            sums.append(jnp.sum(e, axis=0))
            if c + 1 < NK:
                s, high_s = next_s, next_high
        p = peak[half, i]
        best = jnp.max(p, axis=0)
        tops[half, i] = best
        total[half, i] = sum(sums[c] * jnp.exp2((p[c] - best) * SCALE) for c in range(NK))

    def stats():
        return pltpu.make_async_remote_copy(
            src_ref=ml_out,
            dst_ref=ml_in,
            send_sem=st_send.at[2],
            recv_sem=st_recv.at[2],
            device_id=(qp, h),
            device_id_type=MESH,
        )

    def send_stats():
        for i in range(NQ):
            best = jnp.max(jnp.maximum(tops[0, i], tops[1, i]), axis=0, keepdims=True)
            summed = total[0, i] * jnp.exp2((tops[0, i] - best) * SCALE) + total[1, i] * jnp.exp2(
                (tops[1, i] - best) * SCALE
            )
            ml_out[0, i] = best
            ml_out[1, i] = jnp.sum(summed, axis=0, keepdims=True)
        stats().start()

    def take_stats():
        stats().wait()
        for i in range(NQ):
            j = (i + NT) % NQ
            here, there = ml_out[0, i], ml_in[0, j]
            best = jnp.maximum(here, there)
            top[i] = best
            norm[i] = 1.0 / (
                ml_out[1, i] * jnp.exp2((here - best) * SCALE) + ml_in[1, j] * jnp.exp2((there - best) * SCALE)
            )

    def normal(half, i):
        f = jnp.exp2((peak[half, i] - top[i][None]) * SCALE) * norm[i][None]
        e = probs[half, i].astype(jnp.float32).reshape(NK, KC // SUB, SUB, TQ)
        p = (e * f[:, None]).reshape(HALF, TQ).astype(jnp.bfloat16)
        probs[half, i] = p
        return p

    def weight_tile(half, i):
        return dot(v_all[half_rows(half), :], g_all[tile_rows(i), :], CONTRACT_LAST)

    def add_rowdot(i, p, w):
        dsum[i] += jnp.sum((p.astype(jnp.float32) * w).reshape(HALF // SUB, SUB, TQ), axis=0)

    def score_grads(half, i):
        p = probs[half, i].astype(jnp.float32)
        ds = (p * (wgrad[half, i].astype(jnp.float32) - rdot[i])).astype(jnp.bfloat16)
        dk_acc[half] += dot(ds, q_all[tile_rows(i), :], CONTRACT_INNER)
        dq_acc[i] += dot(ds, k_all[half_rows(half), :], CONTRACT_FIRST)

    def share_rowdot(n):
        return pltpu.make_async_remote_copy(
            src_ref=d_out.at[n],
            dst_ref=d_in.at[n],
            send_sem=st_send.at[n],
            recv_sem=st_recv.at[n],
            device_id=(qp, h),
            device_id_type=MESH,
        )

    def partial(n):
        out, into, peer = (
            (dv_send, dv_recv, kp),
            (dk_send, dk_recv, kp),
            (dq_send.at[pl.ds(0, TQ), :], dq_recv.at[pl.ds(0, TQ), :], qp),
            (dq_send.at[pl.ds(TQ, TQ), :], dq_recv.at[pl.ds(TQ, TQ), :], qp),
        )[n]
        return pltpu.make_async_remote_copy(
            src_ref=out,
            dst_ref=into,
            send_sem=part_send.at[n],
            recv_sem=part_recv.at[n],
            device_id=(peer, h),
            device_id_type=MESH,
        )

    def key_part(c):
        rows = pl.ds(c * CR, CR)
        return pltpu.make_async_remote_copy(
            src_ref=dk_send.at[rows, :],
            dst_ref=dk_recv.at[rows, :],
            send_sem=part_send.at[4 + c],
            recv_sem=part_recv.at[4 + c],
            device_id=(kp, h),
            device_id_type=MESH,
        )

    finals = ((dv_send, dv_out), (dk_send, dk_out), (dq_send, dq_out))

    def stay(n):
        fin, out = finals[n]
        return pltpu.make_async_copy(fin.at[pl.ds(0, RB), :], out.at[:, cols(h)], out_local.at[n])

    def spread(n, begin, end):
        fin, out = finals[n]

        def send(p, _):
            peer = lax.rem(h - STRIDE * p + STRIDE * NH, NH)
            pltpu.make_async_remote_copy(
                src_ref=fin.at[block_rows(p), :],
                dst_ref=out.at[:, cols(h)],
                send_sem=out_send.at[n],
                recv_sem=out_recv.at[n],
                device_id=(y, peer),
                device_id_type=MESH,
            ).start()
            return 0

        lax.fori_loop(max(1, begin), end, send, 0)
        if begin == 0:
            stay(n).start()

    for c in range(CHUNKS):
        pass_on(0, c)
        regroup(2, c)
    for c in range(CHUNKS // 2):
        pass_on(1, c)
        regroup(3, c)

    def score_step(t, _):
        half = lax.rem(t // NT, 2)
        i = NT * (t // NQ) + lax.rem(t, NT)

        @pl.when(t == 1)
        def _():
            for c in range(CHUNKS // 2, CHUNKS):
                pass_on(1, c)
                regroup(3, c)

        @pl.when(t == NT)
        def _():
            crossed(0)

        @pl.when(t == NQ)
        def _():
            crossed(1)

        score_tile(half, i)
        for when, a, c in (
            (1, 2, 0), (2, 2, 1), (3, 2, 2), (3, 2, 3),
            (4, 3, 0), (5, 3, 1), (5, 3, 2), (6, 3, 3),
        ):

            @pl.when(t == when)
            def _(a=a, c=c):
                pass_on(a, c)

        return 0

    lax.fori_loop(0, 2 * NQ, score_step, 0)
    send_stats()

    def near_weight_step(i, _):
        @pl.when(i == NT)
        def _():
            crossed(2)

        wgrad[0, i] = weight_tile(0, i).astype(jnp.bfloat16)
        return 0

    lax.fori_loop(0, NQ, near_weight_step, 0)
    take_stats()

    crossed(3)

    def far_step(i, _):
        w = weight_tile(1, i)
        wgrad[1, i] = w.astype(jnp.bfloat16)
        p = normal(1, i)
        add_rowdot(i, p, w)
        dv_acc[...] += dot(p, g_all[tile_rows(i), :], CONTRACT_INNER)
        return 0

    lax.fori_loop(0, NQ, far_step, 0)
    dv_send[...] = dv_acc[...].astype(jnp.bfloat16)
    partial(0).start()
    dv_acc[...] = jnp.zeros_like(dv_acc)

    def near_step(i, _):
        p = normal(0, i)
        add_rowdot(i, p, wgrad[0, i].astype(jnp.float32))
        dv_acc[...] += dot(p, g_all[tile_rows(i), :], CONTRACT_INNER)
        for n in range(2):

            @pl.when(i == NT * n + NT - 1)
            def _(n=n):
                for u in range(NT):
                    d_out[n, u] = jnp.sum(dsum[n * NT + u], axis=0, keepdims=True)
                share_rowdot(n).start()

        return 0

    lax.fori_loop(0, NQ, near_step, 0)

    def take_rowdot(n):
        share_rowdot(n).wait()
        for u in range(NT):
            rdot[(1 - n) * NT + u] = d_out[1 - n, u] + d_in[n, u]

    def finish_queries(i):
        rows = pl.ds(i * TQ, TQ)
        partial(2 + i).wait()
        dq_send[rows, :] = (dq_acc[i] * FACTOR + dq_recv[rows, :].astype(jnp.float32)).astype(jnp.bfloat16)
        spread(2, i * (NH // NT), (i + 1) * (NH // NT))

    def grad_step(t, _):
        half = jnp.where(t < NQ, 1 - lax.rem(t, 2), jnp.where(t < NQ + NT, 1, 0))
        i = jnp.where(t < NQ, NT + t // 2, lax.rem(t, NT))

        @pl.when(t == 0)
        def _():
            take_rowdot(0)

        @pl.when(t == NQ)
        def _():
            take_rowdot(1)

        score_grads(half, i)

        @pl.when(t == 0)
        def _():
            partial(0).wait()
            dv_send[...] = (dv_acc[...] + dv_recv[...].astype(jnp.float32)).astype(jnp.bfloat16)
            spread(0, 0, NH)

        for u in range(NT):

            @pl.when(t == 1 + 2 * u)
            def _(u=u):
                dq_send[pl.ds(u * TQ, TQ), :] = (dq_acc[NT + u] * FACTOR).astype(jnp.bfloat16)
                partial(2 + u).start()

        @pl.when(t == NQ + NT - 1)
        def _():
            dk_send[...] = (dk_acc[1] * FACTOR).astype(jnp.bfloat16)
            for c in range(CHUNKS):
                key_part(c).start()

        for u in range(NT):

            @pl.when(t == NQ + NT + u)
            def _(u=u):
                finish_queries(u)

        return 0

    lax.fori_loop(0, 2 * NQ, grad_step, 0)
    for c in range(CHUNKS):
        rows = pl.ds(c * CR, CR)
        key_part(c).wait()
        dk_send[rows, :] = (dk_acc[0, rows] * FACTOR + dk_recv[rows, :].astype(jnp.float32)).astype(jnp.bfloat16)
        spread(1, c * CB, (c + 1) * CB)

    for a in range(4):
        most = landing[a].at[pl.ds(0, HALF - RB), :]
        pltpu.make_async_copy(most, most, in_send.at[a]).wait()
    for n in range(3):
        fin, out = finals[n]
        sent = fin.at[pl.ds(0, HALF - RB), :]
        came = out.at[:, pl.ds(0, (NH - 1) * HD)]
        stay(n).wait()
        pltpu.make_async_copy(sent, sent, out_send.at[n]).wait()
        pltpu.make_async_copy(came, came, out_recv.at[n]).wait()


def store(dq_in, dk_in, dv_in, dq_out, dk_out, dv_out, sems):
    pairs = ((dq_in, dq_out), (dk_in, dk_out), (dv_in, dv_out))
    copies = [pltpu.make_async_copy(a, b, sems.at[n]) for n, (a, b) in enumerate(pairs)]
    for copy in copies:
        copy.start()
    for copy in copies:
        copy.wait()


def shards(queries, keys, values, grad_out, frame_order, key_blocks, key_count):
    bf16, f32 = jnp.bfloat16, jnp.float32
    half = pltpu.VMEM((HALF, HD), bf16)
    whole = pltpu.VMEM((2 * HALF, HD), bf16)
    tiles = pltpu.VMEM((2, NQ, HALF, TQ), bf16)
    chunk_rows = pltpu.VMEM((2, NQ, NK, SUB, TQ), f32)
    tile_lines = pltpu.VMEM((2, NQ, SUB, TQ), f32)
    line = pltpu.VMEM((NQ, 1, TQ), f32)
    pairs = pltpu.VMEM((2, NQ, 1, TQ), f32)
    pair = pltpu.VMEM((2, NT, 1, TQ), f32)
    dma = pltpu.SemaphoreType.DMA
    anywhere = pl.BlockSpec(memory_space=pl.ANY)
    grads = pl.pallas_call(
        kernel,
        out_shape=[pltpu.VMEM(queries.shape, bf16)] * 3,
        in_specs=[anywhere] * 4
        + [
            pl.BlockSpec(memory_space=pltpu.SMEM),
            pl.BlockSpec(memory_space=pltpu.VMEM),
            pl.BlockSpec(memory_space=pltpu.VMEM),
        ],
        out_specs=[pl.BlockSpec(memory_space=pltpu.VMEM)] * 3,
        scratch_shapes=[whole] * 6
        + [tiles] * 2
        + [chunk_rows, tile_lines, tile_lines]
        + [line, line, pltpu.VMEM((NQ, SUB, TQ), f32), line]
        + [pairs, pairs, pair, pair]
        + [
            pltpu.VMEM((HALF, HD), f32),
            pltpu.VMEM((2, HALF, HD), f32),
            pltpu.VMEM((NQ, TQ, HD), f32),
        ]
        + [half] * 6
        + [
            dma((4,)), dma((4, CHUNKS)), dma((4,)), dma((4, CHUNKS)), dma((4, CHUNKS)),
            dma((3,)), dma((3,)),
            dma((4 + CHUNKS,)), dma((4 + CHUNKS,)), dma((3,)), dma((3,)), dma((3,)),
        ],
        compiler_params=pltpu.CompilerParams(
            collective_id=0, has_side_effects=True, vmem_limit_bytes=62 << 20
        ),
        cost_estimate=pl.CostEstimate(flops=12 * 10**9, bytes_accessed=8 << 20, transcendentals=10**7),
        name="attention_grads",
    )(queries, keys, values, grad_out, frame_order, key_blocks.T, key_count[None, :])
    return pl.pallas_call(
        store,
        out_shape=[jax.ShapeDtypeStruct(queries.shape, bf16)] * 3,
        in_specs=[pl.BlockSpec(memory_space=pltpu.VMEM)] * 3,
        out_specs=[anywhere] * 3,
        scratch_shapes=[dma((3,))],
        compiler_params=pltpu.CompilerParams(vmem_limit_bytes=4 << 20),
        name="store_grads",
    )(*grads)


def solution(mesh):
    tokens = P(("frame", "head"), None)
    return jax.shard_map(
        shards,
        mesh=mesh,
        in_specs=(tokens,) * 4 + (P(),) * 3,
        out_specs=(tokens,) * 3,
        check_vma=False,
    )
```

```python
import jax
import jax.numpy as jnp
from jax import lax
from jax.experimental import pallas as pl
from jax.experimental.pallas import tpu as pltpu
from jax.sharding import PartitionSpec as P

HD = 128
FRAME_TOK = 768
BLK = 128
PER_FRAME = FRAME_TOK // BLK
NH = 32
NY = 4
RB = 48
HALF = NH * RB
CHUNKS = 4
CB = NH // CHUNKS
CR = CB * RB
STRIDE = 5
TQ = 768
NT = HALF // TQ
NQ = 2 * NT
KC = 256
NK = HALF // KC
SUB = 8
GR = 16
FACTOR = HD**-0.5
LOG2E = 1.4426950408889634
SCALE = FACTOR * LOG2E
NEG = -1e30
MESH = pl.DeviceIdType.MESH

CONTRACT_LAST = (((1,), (1,)), ((), ()))
CONTRACT_FIRST = (((0,), (0,)), ((), ()))
CONTRACT_INNER = (((1,), (0,)), ((), ()))


def dot(a, b, dims):
    return lax.dot_general(a, b, dims, preferred_element_type=jnp.float32)


def cols(index):
    return pl.ds(pl.multiple_of(index * HD, HD), HD)


def block_rows(index):
    return pl.ds(pl.multiple_of(index * RB, RB), RB)


def tile_rows(index):
    return pl.ds(pl.multiple_of(index * TQ, TQ), TQ)


def half_rows(index):
    return pl.ds(pl.multiple_of(index * HALF, HALF), HALF)


def kernel(
    q_in, k_in, v_in, g_in, order, lists, counts,
    dq_out, dk_out, dv_out,
    q_all, k_all, v_all, g_all, q_mask, k_mask,
    probs, wgrad, peak, tops, total, top, norm, dsum, rdot,
    ml_out, ml_in, d_out, d_in,
    dv_acc, dk_acc, dq_acc,
    dv_send, dk_send, dq_send, dv_recv, dk_recv, dq_recv,
    in_send, in_recv, in_local, y_send, y_recv, st_send, st_recv,
    part_send, part_recv, out_send, out_recv, out_local,
):
    y = lax.axis_index("frame")
    h = lax.axis_index("head")
    core = lax.rem(h, 2)
    low = y + 1 - 2 * lax.rem(y, 2)
    high = NY - 1 - y
    qp = (1 - core) * low + core * high
    kp = core * low + (1 - core) * high
    barrier = pltpu.get_barrier_semaphore()

    def greet(i, _):
        peer = lax.rem(h + i, NH)
        pl.semaphore_signal(barrier, inc=1, device_id=(y, peer), device_id_type=MESH)
        return 0

    lax.fori_loop(1, NH, greet, 0)
    pl.semaphore_signal(barrier, inc=1, device_id=(qp, h), device_id_type=MESH)
    pl.semaphore_signal(barrier, inc=1, device_id=(kp, h), device_id_type=MESH)
    pl.semaphore_wait(barrier, NH + 1)

    sources = (k_in, q_in, g_in, v_in)
    landing = (k_all, q_all, g_all, v_all)
    partner = (kp, qp, qp, kp)

    def own_block(a):
        return pltpu.make_async_copy(
            sources[a].at[:, cols(h)], landing[a].at[pl.ds(0, RB), :], in_local.at[a]
        )

    def regroup(a, c):
        def send(p, _):
            peer = lax.rem(h + STRIDE * p, NH)
            pltpu.make_async_remote_copy(
                src_ref=sources[a].at[:, cols(peer)],
                dst_ref=landing[a].at[block_rows(p), :],
                send_sem=in_send.at[a],
                recv_sem=in_recv.at[a, c],
                device_id=(y, peer),
                device_id_type=MESH,
            ).start()
            return 0

        lax.fori_loop(max(1, c * CB), (c + 1) * CB, send, 0)

    for a in range(4):
        own_block(a).start()
    for a in range(2):
        for c in range(CHUNKS):
            regroup(a, c)

    def across(a, c):
        return pltpu.make_async_remote_copy(
            src_ref=landing[a].at[pl.ds(c * CR, CR), :],
            dst_ref=landing[a].at[pl.ds(HALF + c * CR, CR), :],
            send_sem=y_send.at[a, c],
            recv_sem=y_recv.at[a, c],
            device_id=(partner[a], h),
            device_id_type=MESH,
        )

    def pass_on(a, c):
        if c == 0:
            own_block(a).wait()
        some = landing[a].at[pl.ds(0, (CB - (c == 0)) * RB), :]
        pltpu.make_async_copy(some, some, in_recv.at[a, c]).wait()
        across(a, c).start()

    def crossed(a):
        for c in range(CHUNKS):
            across(a, c).wait()

    shape = (HALF // GR, HD)
    row = lax.broadcasted_iota(jnp.int32, shape, 0) * GR
    lane = lax.broadcasted_iota(jnp.int32, shape, 1)
    place = row // RB
    holder = lax.rem(h - STRIDE * place + STRIDE * NH, NH)
    stored = holder * RB + row - place * RB
    later = stored >= FRAME_TOK
    spot = jnp.where(later, stored - FRAME_TOK, stored) // BLK

    def one_hot(plane):
        frame = jnp.where(later, order[2 * plane + 1], order[2 * plane])
        return (frame * PER_FRAME + spot == lane).astype(jnp.float32)

    def spell_out(groups):
        return jnp.broadcast_to(groups[:, None, :], (HALF // GR, GR, HD)).reshape(HALF, HD).astype(jnp.bfloat16)

    block_total = lists.shape[1]
    listed = lists[...]
    live = counts[...]
    ids = lax.broadcasted_iota(jnp.int32, (HD, block_total), 0)
    barred = jnp.full((HD, block_total), NEG, jnp.float32)
    for j in range(lists.shape[0]):
        barred = jnp.where((listed[j : j + 1, :] == ids) & (live > j), 0.0, barred)
    mine = one_hot(y)
    k_mask[pl.ds(0, HALF), :] = spell_out(mine)
    k_mask[pl.ds(HALF, HALF), :] = spell_out(one_hot(kp))
    for half, hot in ((0, mine), (1, one_hot(qp))):
        q_mask[pl.ds(half * HALF, HALF), :] = spell_out(dot(hot[:, :block_total], barred, CONTRACT_LAST))
    dv_acc[...] = jnp.zeros_like(dv_acc)
    dk_acc[...] = jnp.zeros_like(dk_acc)
    dq_acc[...] = jnp.zeros_like(dq_acc)
    dsum[...] = jnp.zeros_like(dsum)

    def score_tile(half, i):
        q = jnp.concatenate([q_all[tile_rows(i), :], q_mask[tile_rows(i), :]], axis=1)

        def scores(c):
            keys = pl.ds(pl.multiple_of(half * HALF + c * KC, KC), KC)
            k = jnp.concatenate([k_all[keys, :], k_mask[keys, :]], axis=1)
            s = dot(k, q, CONTRACT_LAST).reshape(KC // SUB, SUB, TQ)
            return s, jnp.max(s, axis=0)

        s, high_s = scores(0)
        sums = []
        for c in range(NK):
            if c + 1 < NK:
                next_s, next_high = scores(c + 1)
            e = jnp.exp2((s - high_s[None]) * SCALE)
            probs[half, i, pl.ds(c * KC, KC)] = e.reshape(KC, TQ).astype(jnp.bfloat16)
            peak[half, i, c] = high_s
            sums.append(jnp.sum(e, axis=0))
            if c + 1 < NK:
                s, high_s = next_s, next_high
        p = peak[half, i]
        best = jnp.max(p, axis=0)
        tops[half, i] = best
        total[half, i] = sum(sums[c] * jnp.exp2((p[c] - best) * SCALE) for c in range(NK))

    def stats():
        return pltpu.make_async_remote_copy(
            src_ref=ml_out,
            dst_ref=ml_in,
            send_sem=st_send.at[2],
            recv_sem=st_recv.at[2],
            device_id=(qp, h),
            device_id_type=MESH,
        )

    def send_stats():
        for i in range(NQ):
            best = jnp.max(jnp.maximum(tops[0, i], tops[1, i]), axis=0, keepdims=True)
            summed = total[0, i] * jnp.exp2((tops[0, i] - best) * SCALE) + total[1, i] * jnp.exp2(
                (tops[1, i] - best) * SCALE
            )
            ml_out[0, i] = best
            ml_out[1, i] = jnp.sum(summed, axis=0, keepdims=True)
        stats().start()

    def take_stats():
        stats().wait()
        for i in range(NQ):
            j = (i + NT) % NQ
            here, there = ml_out[0, i], ml_in[0, j]
            best = jnp.maximum(here, there)
            top[i] = best
            norm[i] = 1.0 / (
                ml_out[1, i] * jnp.exp2((here - best) * SCALE) + ml_in[1, j] * jnp.exp2((there - best) * SCALE)
            )

    def normal(half, i):
        f = jnp.exp2((peak[half, i] - top[i][None]) * SCALE) * norm[i][None]
        e = probs[half, i].astype(jnp.float32).reshape(NK, KC // SUB, SUB, TQ)
        p = (e * f[:, None]).reshape(HALF, TQ)
        rounded = p.astype(jnp.bfloat16)
        probs[half, i] = rounded
        return p, rounded

    def weight_tile(half, i):
        return dot(v_all[half_rows(half), :], g_all[tile_rows(i), :], CONTRACT_LAST)

    def add_rowdot(i, p, w):
        dsum[i] += jnp.sum((p * w).reshape(HALF // SUB, SUB, TQ), axis=0)

    def score_grads(half, i):
        ds = probs[half, i] * (wgrad[half, i].astype(jnp.float32) - rdot[i]).astype(jnp.bfloat16)
        dk_acc[half] += dot(ds, q_all[tile_rows(i), :], CONTRACT_INNER)
        dq_acc[i] += dot(ds, k_all[half_rows(half), :], CONTRACT_FIRST)

    def share_rowdot(n):
        return pltpu.make_async_remote_copy(
            src_ref=d_out.at[n],
            dst_ref=d_in.at[n],
            send_sem=st_send.at[n],
            recv_sem=st_recv.at[n],
            device_id=(qp, h),
            device_id_type=MESH,
        )

    def partial(n):
        out, into, peer = (
            (dv_send, dv_recv, kp),
            (dk_send, dk_recv, kp),
            (dq_send.at[pl.ds(0, TQ), :], dq_recv.at[pl.ds(0, TQ), :], qp),
            (dq_send.at[pl.ds(TQ, TQ), :], dq_recv.at[pl.ds(TQ, TQ), :], qp),
        )[n]
        return pltpu.make_async_remote_copy(
            src_ref=out,
            dst_ref=into,
            send_sem=part_send.at[n],
            recv_sem=part_recv.at[n],
            device_id=(peer, h),
            device_id_type=MESH,
        )

    def key_part(c):
        rows = pl.ds(c * CR, CR)
        return pltpu.make_async_remote_copy(
            src_ref=dk_send.at[rows, :],
            dst_ref=dk_recv.at[rows, :],
            send_sem=part_send.at[4 + c],
            recv_sem=part_recv.at[4 + c],
            device_id=(kp, h),
            device_id_type=MESH,
        )

    finals = ((dv_send, dv_out), (dk_send, dk_out), (dq_send, dq_out))

    def stay(n):
        fin, out = finals[n]
        return pltpu.make_async_copy(fin.at[pl.ds(0, RB), :], out.at[:, cols(h)], out_local.at[n])

    def spread(n, begin, end):
        fin, out = finals[n]

        def send(p, _):
            peer = lax.rem(h - STRIDE * p + STRIDE * NH, NH)
            pltpu.make_async_remote_copy(
                src_ref=fin.at[block_rows(p), :],
                dst_ref=out.at[:, cols(h)],
                send_sem=out_send.at[n],
                recv_sem=out_recv.at[n],
                device_id=(y, peer),
                device_id_type=MESH,
            ).start()
            return 0

        lax.fori_loop(max(1, begin), end, send, 0)
        if begin == 0:
            stay(n).start()

    for c in range(CHUNKS):
        pass_on(0, c)
        regroup(2, c)
    for c in range(CHUNKS // 2):
        pass_on(1, c)
        regroup(3, c)

    def score_step(t, _):
        half = lax.rem(t // NT, 2)
        i = NT * (t // NQ) + lax.rem(t, NT)

        @pl.when(t == 1)
        def _():
            for c in range(CHUNKS // 2, CHUNKS):
                pass_on(1, c)
                regroup(3, c)

        @pl.when(t == NT)
        def _():
            crossed(0)

        @pl.when(t == NQ)
        def _():
            crossed(1)

        score_tile(half, i)
        for when, a, c in (
            (1, 2, 0), (2, 2, 1), (3, 2, 2), (3, 2, 3),
            (4, 3, 0), (5, 3, 1), (5, 3, 2), (6, 3, 3),
        ):

            @pl.when(t == when)
            def _(a=a, c=c):
                pass_on(a, c)

        return 0

    lax.fori_loop(0, 2 * NQ, score_step, 0)
    send_stats()

    def near_weight_step(i, _):
        @pl.when(i == NT)
        def _():
            crossed(2)

        wgrad[0, i] = weight_tile(0, i).astype(jnp.bfloat16)
        return 0

    lax.fori_loop(0, NQ, near_weight_step, 0)
    take_stats()

    crossed(3)

    def far_step(i, _):
        w = weight_tile(1, i)
        wgrad[1, i] = w.astype(jnp.bfloat16)
        p, rounded = normal(1, i)
        add_rowdot(i, p, w)
        dv_acc[...] += dot(rounded, g_all[tile_rows(i), :], CONTRACT_INNER)
        return 0

    lax.fori_loop(0, NQ, far_step, 0)
    dv_send[...] = dv_acc[...].astype(jnp.bfloat16)
    partial(0).start()
    dv_acc[...] = jnp.zeros_like(dv_acc)

    def near_step(i, _):
        p, rounded = normal(0, i)
        add_rowdot(i, p, wgrad[0, i].astype(jnp.float32))
        dv_acc[...] += dot(rounded, g_all[tile_rows(i), :], CONTRACT_INNER)
        for n in range(2):

            @pl.when(i == NT * n + NT - 1)
            def _(n=n):
                for u in range(NT):
                    d_out[n, u] = jnp.sum(dsum[n * NT + u], axis=0, keepdims=True)
                share_rowdot(n).start()

        return 0

    lax.fori_loop(0, NQ, near_step, 0)

    def take_rowdot(n):
        share_rowdot(n).wait()
        for u in range(NT):
            rdot[(1 - n) * NT + u] = d_out[1 - n, u] + d_in[n, u]

    def finish_queries(i):
        rows = pl.ds(i * TQ, TQ)
        partial(2 + i).wait()
        dq_send[rows, :] = (dq_acc[i] * FACTOR + dq_recv[rows, :].astype(jnp.float32)).astype(jnp.bfloat16)
        spread(2, i * (NH // NT), (i + 1) * (NH // NT))

    def grad_step(t, _):
        half = jnp.where(t < NQ, 1 - lax.rem(t, 2), jnp.where(t < NQ + NT, 1, 0))
        i = jnp.where(t < NQ, NT + t // 2, lax.rem(t, NT))

        @pl.when(t == 0)
        def _():
            take_rowdot(0)

        @pl.when(t == NQ)
        def _():
            take_rowdot(1)

        score_grads(half, i)

        for u in range(NT):

            @pl.when(t == 1 + 2 * u)
            def _(u=u):
                dq_send[pl.ds(u * TQ, TQ), :] = (dq_acc[NT + u] * FACTOR).astype(jnp.bfloat16)
                partial(2 + u).start()

        @pl.when(t == 3)
        def _():
            partial(0).wait()
            dv_send[...] = (dv_acc[...] + dv_recv[...].astype(jnp.float32)).astype(jnp.bfloat16)
            spread(0, 0, NH)

        @pl.when(t == NQ + NT - 1)
        def _():
            dk_send[...] = (dk_acc[1] * FACTOR).astype(jnp.bfloat16)
            for c in range(CHUNKS):
                key_part(c).start()

        for u in range(NT):

            @pl.when(t == NQ + NT + u)
            def _(u=u):
                finish_queries(u)

        return 0

    lax.fori_loop(0, 2 * NQ, grad_step, 0)
    for c in range(CHUNKS):
        rows = pl.ds(c * CR, CR)
        key_part(c).wait()
        dk_send[rows, :] = (dk_acc[0, rows] * FACTOR + dk_recv[rows, :].astype(jnp.float32)).astype(jnp.bfloat16)
        spread(1, c * CB, (c + 1) * CB)

    for a in range(4):
        most = landing[a].at[pl.ds(0, HALF - RB), :]
        pltpu.make_async_copy(most, most, in_send.at[a]).wait()
    for n in range(3):
        fin, out = finals[n]
        sent = fin.at[pl.ds(0, HALF - RB), :]
        came = out.at[:, pl.ds(0, (NH - 1) * HD)]
        stay(n).wait()
        pltpu.make_async_copy(sent, sent, out_send.at[n]).wait()
        pltpu.make_async_copy(came, came, out_recv.at[n]).wait()


def store(dq_in, dk_in, dv_in, dq_out, dk_out, dv_out, sems):
    pairs = ((dq_in, dq_out), (dk_in, dk_out), (dv_in, dv_out))
    copies = [pltpu.make_async_copy(a, b, sems.at[n]) for n, (a, b) in enumerate(pairs)]
    for copy in copies:
        copy.start()
    for copy in copies:
        copy.wait()


def shards(queries, keys, values, grad_out, frame_order, key_blocks, key_count):
    bf16, f32 = jnp.bfloat16, jnp.float32
    half = pltpu.VMEM((HALF, HD), bf16)
    whole = pltpu.VMEM((2 * HALF, HD), bf16)
    tiles = pltpu.VMEM((2, NQ, HALF, TQ), bf16)
    chunk_rows = pltpu.VMEM((2, NQ, NK, SUB, TQ), f32)
    tile_lines = pltpu.VMEM((2, NQ, SUB, TQ), f32)
    line = pltpu.VMEM((NQ, 1, TQ), f32)
    pairs = pltpu.VMEM((2, NQ, 1, TQ), f32)
    pair = pltpu.VMEM((2, NT, 1, TQ), f32)
    dma = pltpu.SemaphoreType.DMA
    anywhere = pl.BlockSpec(memory_space=pl.ANY)
    grads = pl.pallas_call(
        kernel,
        out_shape=[pltpu.VMEM(queries.shape, bf16)] * 3,
        in_specs=[anywhere] * 4
        + [
            pl.BlockSpec(memory_space=pltpu.SMEM),
            pl.BlockSpec(memory_space=pltpu.VMEM),
            pl.BlockSpec(memory_space=pltpu.VMEM),
        ],
        out_specs=[pl.BlockSpec(memory_space=pltpu.VMEM)] * 3,
        scratch_shapes=[whole] * 6
        + [tiles] * 2
        + [chunk_rows, tile_lines, tile_lines]
        + [line, line, pltpu.VMEM((NQ, SUB, TQ), f32), line]
        + [pairs, pairs, pair, pair]
        + [
            pltpu.VMEM((HALF, HD), f32),
            pltpu.VMEM((2, HALF, HD), f32),
            pltpu.VMEM((NQ, TQ, HD), f32),
        ]
        + [half] * 6
        + [
            dma((4,)), dma((4, CHUNKS)), dma((4,)), dma((4, CHUNKS)), dma((4, CHUNKS)),
            dma((3,)), dma((3,)),
            dma((4 + CHUNKS,)), dma((4 + CHUNKS,)), dma((3,)), dma((3,)), dma((3,)),
        ],
        compiler_params=pltpu.CompilerParams(
            collective_id=0, has_side_effects=True, vmem_limit_bytes=62 << 20
        ),
        cost_estimate=pl.CostEstimate(flops=12 * 10**9, bytes_accessed=8 << 20, transcendentals=10**7),
        name="attention_grads",
    )(queries, keys, values, grad_out, frame_order, key_blocks.T, key_count[None, :])
    return pl.pallas_call(
        store,
        out_shape=[jax.ShapeDtypeStruct(queries.shape, bf16)] * 3,
        in_specs=[pl.BlockSpec(memory_space=pltpu.VMEM)] * 3,
        out_specs=[anywhere] * 3,
        scratch_shapes=[dma((3,))],
        compiler_params=pltpu.CompilerParams(vmem_limit_bytes=4 << 20),
        name="store_grads",
    )(*grads)


def solution(mesh):
    tokens = P(("frame", "head"), None)
    return jax.shard_map(
        shards,
        mesh=mesh,
        in_specs=(tokens,) * 4 + (P(),) * 3,
        out_specs=(tokens,) * 3,
        check_vma=False,
    )
```
